256 devices in a mesh: seq: 32 (over y, x, core), head: 8 (over z).
Axes of the slice: x: 4, y: 4, z: 8, core: 2. Of those that a mesh axis runs over, the one named last changes fastest.
Arguments:
- queries: bfloat16 [6144, 2048], P('seq', 'head'), may hold values from -6 to 6
- key_states: bfloat16 [6144, 2048], P('seq', 'head'), may hold values from -6 to 6
- value_states: bfloat16 [6144, 2048], P('seq', 'head'), may hold values from -6 to 6
- w_out: bfloat16 [2048, 4096], P('head'), may hold values from -0.125 to 0.125
- grad_y: bfloat16 [6144, 4096], P('seq'), may hold values from -6 to 6
- chain_order: int32 [32], replicated, may hold values from 0 to 31, each once
Outputs:
- layer_out: bfloat16 [6144, 4096], P('seq', 'head')
- grad_queries: bfloat16 [6144, 2048], P('seq', 'head')
- grad_keys: bfloat16 [6144, 2048], P('seq', 'head')
- grad_values: bfloat16 [6144, 2048], P('seq', 'head')
- grad_weight: bfloat16 [2048, 4096], P('head', 'seq')
The draws below stay inside these ranges and needn't reach their ends.
Inputs may be any that keep to these rules, and one draw needn't show every extreme that they name: chain_order names each of 0 to 31 once.
All inputs are finite; a program needn't handle non-finite values.
Results may differ from the reference program's by a relative error of at most 0.025.
Values may be sent and summed in bfloat16 or wider, within the bound.
A program may use at most 64 MiB of HBM per device.

```python
import math
import jax
import jax.numpy as jnp
from jax import lax

D = 4096
HEADS = 16
HEAD_DIM = 128
TOK_DEV = 192
TOKENS = 6144
N_SEQ = 32
N_HEAD = 8


def shared_pattern(key):
    shape = (TOKENS, HEADS * HEAD_DIM)
    signs = jnp.where(jax.random.bernoulli(key, 0.5, shape), 1.0, -1.0).astype(jnp.float32)
    return signs


def draw_queries(key, part):
    signs = shared_pattern(key)
    key = jax.random.fold_in(key, 11)
    result = jnp.clip(jax.random.normal(key, signs.shape, jnp.float32), -6.0, 6.0)
    return result.astype(jnp.bfloat16)


def draw_key_states(key, part):
    signs = shared_pattern(key)
    key = jax.random.fold_in(key, 12)
    result = jnp.clip(jax.random.normal(key, signs.shape, jnp.float32), -6.0, 6.0)
    return result.astype(jnp.bfloat16)


def raised(entries, own_key, source, target, shards_of, factor):
    def block_of(dim):
        return (jnp.arange(entries.shape[dim]) // (entries.shape[dim] // shards_of)).reshape((-1,) + (1,) * (entries.ndim - 1 - dim))

    one_side = jax.random.permutation(own_key, shards_of)[block_of(target)]
    far = (block_of(target) + shards_of // 2) % shards_of
    return jnp.where((block_of(source) == one_side) | (block_of(source) == far), factor * entries, entries)


def shard_levels(key, dims, split, smallest, top_value):
    level = 1.0
    for position, shards_of in split:
        draws = jax.random.uniform(jax.random.fold_in(jax.random.fold_in(key, 6), position), (shards_of,), jnp.float32, smallest / len(split), top_value / len(split))
        level = level * jnp.repeat(jnp.exp(draws), dims[position] // shards_of).reshape((-1,) + (1,) * (len(dims) - 1 - position))
    return level


def normal_values(stream_key, extent, spread, reach, shards=(), kind=jnp.bfloat16):
    array = jax.random.normal(stream_key, extent, jnp.float32) * spread
    if len(shards) > 0:
        array = shard_levels(stream_key, extent, shards, -0.22, 0.18) * array
    return jnp.clip(array, min=-reach, max=reach).astype(kind)


def gaussian_with(stream_key, dims, deviation, reach, pieces, heavy, kind=jnp.bfloat16):
    values = deviation * jax.random.normal(stream_key, dims, jnp.float32)
    if pieces:
        values = values * shard_levels(stream_key, dims, pieces, -0.22, 0.18)
    return jnp.clip(raised(values, jax.random.fold_in(stream_key, 3), *heavy), -reach, reach).astype(kind)


def setup_inputs(seed: int = 0) -> dict:
    keys = jax.random.split(jax.random.key(seed), 7)
    queries = draw_queries(jax.random.fold_in(keys[6], 71), 0)
    key_states = draw_key_states(jax.random.fold_in(keys[6], 71), 0)
    value_states = normal_values(keys[2], (TOKENS, HEADS * HEAD_DIM), 1.0, 6.0, ((0, 32), (1, 8)))
    w_out = normal_values(keys[3], (HEADS * HEAD_DIM, D), (HEADS * HEAD_DIM) ** -0.5, 0.125, ((0, 8),))
    grad_y = gaussian_with(keys[4], (TOKENS, D), 1.0, 6.0, ((0, 32),), (0, 1, 32, 2.75))
    chain_order = jax.random.permutation(keys[5], N_SEQ).astype(jnp.int32)
    return dict(queries=queries, key_states=key_states, value_states=value_states, w_out=w_out, grad_y=grad_y, chain_order=chain_order)


def reference(queries, key_states, value_states, w_out, grad_y, chain_order):
    rows = jnp.arange(TOKENS, dtype=jnp.int32)
    positions = chain_order[rows // TOK_DEV].astype(jnp.int32) * TOK_DEV + rows % TOK_DEV
    allowed = positions[None, :] <= positions[:, None]
    score_scale = 1.0 / math.sqrt(HEAD_DIM)

    def by_head(matrix):
        return matrix.reshape(TOKENS, HEADS, HEAD_DIM).transpose(1, 0, 2)
    q_heads = by_head(queries)
    k_heads = by_head(key_states)
    v_heads = by_head(value_states)

    def scores_of(q_one, k_one):
        raw = jnp.dot(q_one, k_one.T, preferred_element_type=jnp.float32) * score_scale
        return jnp.where(allowed, raw, -jnp.inf)

    def forward_head(members):
        q_one, k_one, v_one = members
        scores = scores_of(q_one, k_one)
        running = lax.optimization_barrier(jnp.max(scores, axis=1))
        weights = jnp.exp(scores - running[:, None])
        denominator = lax.optimization_barrier(jnp.sum(weights, axis=1))
        summed = jnp.dot(weights.astype(jnp.bfloat16), v_one, preferred_element_type=jnp.float32)
        return ((summed / denominator[:, None]).astype(jnp.bfloat16), running + jnp.log(denominator))
    attention, log_norm = lax.map(forward_head, (q_heads, k_heads, v_heads))
    attention_rows = attention.transpose(1, 0, 2).reshape(TOKENS, HEADS * HEAD_DIM)
    group_cols = HEADS * HEAD_DIM // N_HEAD
    total_out = jnp.zeros((TOKENS, D), jnp.float32)
    for group in range(N_HEAD):
        group_out = jnp.dot(attention_rows[:, group * group_cols:(group + 1) * group_cols], w_out[group * group_cols:(group + 1) * group_cols], preferred_element_type=jnp.float32).astype(jnp.bfloat16)
        group_out = lax.optimization_barrier(group_out)
        total_out = total_out + group_out.astype(jnp.float32)
    layer_out = total_out.astype(jnp.bfloat16)
    grad_attention = jnp.dot(grad_y, w_out.T, preferred_element_type=jnp.float32).astype(jnp.bfloat16)
    grad_weight = jnp.dot(attention_rows.T, grad_y, preferred_element_type=jnp.float32).astype(jnp.bfloat16)
    d_heads = by_head(grad_attention)
    delta = lax.optimization_barrier(jnp.sum(d_heads.astype(jnp.float32) * attention.astype(jnp.float32), axis=2))

    def backward_head(members):
        q_one, k_one, v_one, d_one, norm_one, delta_one = members
        scores = scores_of(q_one, k_one)
        probs = jnp.exp(scores - norm_one[:, None])
        grad_v = jnp.dot(probs.astype(jnp.bfloat16).T, d_one, preferred_element_type=jnp.float32)
        slopes = jnp.dot(d_one, v_one.T, preferred_element_type=jnp.float32)
        dscores = (probs * (slopes - delta_one[:, None])).astype(jnp.bfloat16)
        grad_q = jnp.dot(dscores, k_one, preferred_element_type=jnp.float32) * score_scale
        grad_k = jnp.dot(dscores.T, q_one, preferred_element_type=jnp.float32) * score_scale
        return (grad_q.astype(jnp.bfloat16), grad_k.astype(jnp.bfloat16), grad_v.astype(jnp.bfloat16))
    grad_q, grad_k, grad_v = lax.map(backward_head, (q_heads, k_heads, v_heads, d_heads, log_norm, delta))

    def merged(stacked):
        return stacked.transpose(1, 0, 2).reshape(TOKENS, HEADS * HEAD_DIM)
    return (layer_out, merged(grad_q), merged(grad_k), merged(grad_v), grad_weight)
```

```python
import math

import jax
import jax.numpy as jnp
from jax import lax
from jax.experimental import pallas as pl
from jax.experimental.pallas import tpu as pltpu
from jax.sharding import PartitionSpec as P

F32 = jnp.float32
BF16 = jnp.bfloat16
MESH = pl.DeviceIdType.MESH
HEAD = 128
TOK = 192
CHIP = 2 * TOK
HALF = TOK // 2
N_Z = 8
SCALE = 1.0 / math.sqrt(HEAD)
SCALE2 = SCALE * math.log2(math.e)
NEG = -1e30

RIGHT, LEFT, DOWN, UP = (0, 1), (0, -1), (1, 0), (-1, 0)
EVEN, ODD = (0, TOK), (TOK, TOK)
EVEN_TOP, EVEN_LOW = (0, HALF), (HALF, HALF)
ODD_TOP, ODD_LOW = (TOK, HALF), (TOK + HALF, HALF)
WHOLE = (0, CHIP)

HOPS = [
    [((0, 0), WHOLE, d) for d in (RIGHT, LEFT, DOWN, UP)],
    [
        ((0, -1), EVEN, RIGHT),
        ((0, -1), EVEN, DOWN),
        ((0, -1), EVEN, UP),
        ((0, 1), ODD, LEFT),
        ((0, 1), EVEN, DOWN),
        ((0, 1), EVEN, UP),
        ((-1, 0), EVEN, DOWN),
        ((-1, 0), ODD, RIGHT),
        ((-1, 0), ODD, LEFT),
        ((1, 0), ODD, UP),
        ((1, 0), ODD, RIGHT),
        ((1, 0), ODD, LEFT),
    ],
    [
        ((0, 2), EVEN, DOWN),
        ((0, 2), EVEN, UP),
        ((2, 0), ODD, RIGHT),
        ((2, 0), ODD, LEFT),
        ((-1, -1), EVEN_TOP, DOWN),
        ((-1, 1), EVEN_TOP, DOWN),
        ((1, -1), EVEN_LOW, UP),
        ((1, 1), EVEN_LOW, UP),
        ((-1, -1), ODD_TOP, RIGHT),
        ((1, -1), ODD_TOP, RIGHT),
        ((-1, 1), ODD_LOW, LEFT),
        ((1, 1), ODD_LOW, LEFT),
    ],
    [
        ((-1, 2), EVEN_TOP, DOWN),
        ((1, 2), EVEN_LOW, UP),
        ((2, -1), ODD_TOP, RIGHT),
        ((2, 1), ODD_LOW, LEFT),
    ],
]
FIRST = [0, 4, 16, 28]
N_COPIES = 32
GROUPS = [
    [(0, 0), (0, -1), (0, 1), (-1, 0), (1, 0)],
    [(0, 2), (2, 0), (-1, -1), (-1, 1), (1, -1), (1, 1)],
    [(-1, 2), (1, 2), (2, -1), (2, 1), (2, 2)],
]


def dot(a, b):
    return jnp.dot(a, b, preferred_element_type=F32)


def dot_nt(a, b):
    return lax.dot_general(a, b, (((1,), (1,)), ((), ())), preferred_element_type=F32)


def wrap(value, size):
    return lax.rem(value + 2 * size, size)


def kernel(
    q_hbm, k_hbm, v_hbm, w_hbm, gy_hbm, order,
    out_ref, dq_ref, dk_ref, dv_ref, gw_ref,
    kv, qd, wv, gyc, wc, ag, gb, r1, h1, r2, gf, st, attb, dstage, swap, gswap,
    m, l, acc, dq, dk, dv,
    kv_s, kv_r, qd_s, qd_r, loc, sib_s, sib_r, wz_s, wz_r, ws_s, ws_r, st_s, st_r,
    az_s, az_r, g1_s, g1_r, g2_s, g2_r,
):
    s = lax.axis_index("seq")
    z = lax.axis_index("head")
    y = s // 8
    x = lax.rem(s // 2, 4)
    c = lax.rem(s, 2)
    chip = y * 4 + x
    twin = (s + 1 - 2 * c, z)
    o = 1 - c

    def at(step):
        return ((wrap(y + step[0], 4) * 4 + wrap(x + step[1], 4)) * 2 + c, z)

    def chip_at(step):
        return wrap(y + step[0], 4) * 4 + wrap(x + step[1], 4)

    def rows(step, part=WHOLE):
        return pl.ds(pl.multiple_of(chip_at(step) * CHIP + part[0], 32), part[1])

    def cols(index, size=HEAD):
        return pl.ds(pl.multiple_of(index * size, size), size)

    def remote(src, dst, send, recv, device):
        return pltpu.make_async_remote_copy(
            src_ref=src, dst_ref=dst, send_sem=send, recv_sem=recv, device_id=device, device_id_type=MESH
        )

    sent = []

    def send(src, dst, ssem, rsem, device):
        copy = remote(src, dst, ssem, rsem, device)
        copy.start()
        sent.append(copy)

    def arrived(dst, ssem, rsem):
        remote(dst, dst, ssem, rsem, twin).wait_recv()

    def hop_send(buf, ssem, rsem, hop, which):
        for i in which:
            step, part, way = HOPS[hop][i]
            place = buf.at[rows(step, part)]
            n = FIRST[hop] + i
            send(place, place, ssem.at[n], rsem.at[n], at(way))

    def hop_wait(buf, ssem, rsem, hop, which):
        for i in which:
            step, part, way = HOPS[hop][i]
            place = buf.at[rows((step[0] - way[0], step[1] - way[1]), part)]
            n = FIRST[hop] + i
            arrived(place, ssem.at[n], rsem.at[n])

    mine = pl.ds(pl.multiple_of(s * TOK, 32), TOK)
    half = pl.ds(pl.multiple_of(c * TOK, 32), TOK)
    other_half = pl.ds(pl.multiple_of(o * TOK, 32), TOK)
    local = [
        pltpu.make_async_copy(k_hbm.at[:, cols(c)], kv.at[mine, 0:HEAD], loc.at[0]),
        pltpu.make_async_copy(v_hbm.at[:, cols(c)], kv.at[mine, HEAD : 2 * HEAD], loc.at[1]),
        pltpu.make_async_copy(q_hbm.at[:, cols(c)], qd.at[mine, 0:HEAD], loc.at[2]),
        pltpu.make_async_copy(w_hbm, wv, loc.at[3]),
        pltpu.make_async_copy(gy_hbm, gyc.at[half], loc.at[4]),
        pltpu.make_async_copy(w_hbm.at[:, cols(z, 512)], wc.at[z], loc.at[5]),
    ]
    for copy in local:
        copy.start()
    m[...] = jnp.full_like(m, NEG)
    for ref in (l, acc, dq, dk, dv):
        ref[...] = jnp.zeros_like(ref)

    barrier = pltpu.get_barrier_semaphore()
    peers = [twin]
    for d in (1, 2, 3):
        peers += [at((0, d)), at((d, 0))]
    for d in range(1, N_Z):
        peers.append((s, wrap(z + d, N_Z)))
    for peer in peers:
        pl.semaphore_signal(barrier, inc=1, device_id=peer, device_id_type=MESH)
    pl.semaphore_wait(barrier, len(peers))

    send(k_hbm.at[:, cols(o)], kv.at[mine, 0:HEAD], sib_s.at[0], sib_r.at[0], twin)
    send(v_hbm.at[:, cols(o)], kv.at[mine, HEAD : 2 * HEAD], sib_s.at[1], sib_r.at[1], twin)
    send(q_hbm.at[:, cols(o)], qd.at[mine, 0:HEAD], sib_s.at[2], sib_r.at[2], twin)
    theirs = pl.ds(pl.multiple_of((s + 1 - 2 * c) * TOK, 32), TOK)
    local[0].wait()
    local[1].wait()
    arrived(kv.at[theirs, 0:HEAD], sib_s.at[0], sib_r.at[0])
    arrived(kv.at[theirs, HEAD : 2 * HEAD], sib_s.at[1], sib_r.at[1])
    hop_send(kv, kv_s, kv_r, 0, range(4))
    for d in range(1, N_Z):
        far = wrap(z + d, N_Z)
        send(
            w_hbm.at[cols(c), cols(far, 512)], wc.at[z, cols(c)], wz_s.at[d - 1], wz_r.at[d - 1], (s, far)
        )
    send(gy_hbm, gyc.at[half], sib_s.at[4], sib_r.at[4], twin)

    local[3].wait()
    local[4].wait()
    d_own = dot_nt(gyc[half, :], wv[...]).astype(BF16)
    dstage[0] = jnp.where(c == 0, d_own[:, 0:HEAD], d_own[:, HEAD:])
    dstage[1] = jnp.where(c == 0, d_own[:, HEAD:], d_own[:, 0:HEAD])
    qd[mine, HEAD : 2 * HEAD] = dstage[0]
    send(dstage.at[1], qd.at[mine, HEAD : 2 * HEAD], sib_s.at[3], sib_r.at[3], twin)

    def block_pos(index):
        return order[index] * TOK

    def row_pos(chips):
        lane = lax.broadcasted_iota(jnp.int32, (1, CHIP), 1)
        parts = [
            jnp.where(lane < TOK, block_pos(2 * n), block_pos(2 * n + 1) - TOK) + lane for n in chips
        ]
        return jnp.concatenate(parts, axis=1)

    def col_pos(a):
        return lax.broadcasted_iota(jnp.int32, (TOK, 1), 0) + block_pos(2 * chip + a)

    def own_rows(a):
        return pl.ds(pl.multiple_of(chip * CHIP + a * TOK, 32), TOK)

    def chip_rows(n):
        return pl.ds(pl.multiple_of(n * CHIP, 128), CHIP)

    def forward(chips):
        keys = jnp.concatenate([kv[chip_rows(n), 0:HEAD] for n in chips], axis=0)
        values = jnp.concatenate([kv[chip_rows(n), HEAD : 2 * HEAD] for n in chips], axis=0)
        key_pos = row_pos(chips)
        for a in range(2):
            rs = slice(a * TOK, (a + 1) * TOK)
            scores = dot_nt(qd[own_rows(a), 0:HEAD], keys) * SCALE2
            scores = jnp.where(key_pos <= col_pos(a), scores, NEG)
            before = m[rs, 0:1]
            now = jnp.maximum(before, jnp.max(scores, axis=1, keepdims=True))
            factor = jnp.exp2(before - now)
            weights = jnp.exp2(scores - now)
            m[rs, :] = jnp.broadcast_to(now, (TOK, HEAD))
            total = weights[:, 0:HEAD]
            for t in range(1, weights.shape[1] // HEAD):
                total = total + weights[:, t * HEAD : (t + 1) * HEAD]
            l[rs, :] = l[rs, :] * factor + total
            acc[rs, :] = acc[rs, :] * factor + dot(weights.astype(BF16), values)

    def query_grad(chips):
        keys = jnp.concatenate([kv[chip_rows(n), 0:HEAD] for n in chips], axis=0)
        values = jnp.concatenate([kv[chip_rows(n), HEAD : 2 * HEAD] for n in chips], axis=0)
        key_pos = row_pos(chips)
        for a in range(2):
            rs = slice(a * TOK, (a + 1) * TOK)
            scores = dot_nt(qd[own_rows(a), 0:HEAD], keys) * SCALE2 - m[rs, 0:1]
            probs = jnp.exp2(jnp.where(key_pos <= col_pos(a), scores, NEG))
            slopes = dot_nt(qd[own_rows(a), HEAD : 2 * HEAD], values)
            dscore = (probs * (slopes - l[rs, 0:1])).astype(BF16)
            dq[rs, :] += dot(dscore, keys)

    def key_grad(chips):
        queries = jnp.concatenate([qd[chip_rows(n), 0:HEAD] for n in chips], axis=0)
        douts = jnp.concatenate([qd[chip_rows(n), HEAD : 2 * HEAD] for n in chips], axis=0)
        query_pos = row_pos(chips)
        norm = jnp.concatenate([st[n, 0:1, :] for n in chips], axis=1)
        delta = jnp.concatenate([st[n, 1:2, :] for n in chips], axis=1)
        for a in range(2):
            rs = slice(a * TOK, (a + 1) * TOK)
            scores = dot_nt(kv[own_rows(a), 0:HEAD], queries) * SCALE2 - norm
            probs = jnp.exp2(jnp.where(col_pos(a) <= query_pos, scores, NEG))
            dv[rs, :] += dot(probs.astype(BF16), douts)
            slopes = dot_nt(kv[own_rows(a), HEAD : 2 * HEAD], douts)
            dscore = (probs * (slopes - delta)).astype(BF16)
            dk[rs, :] += dot(dscore, queries)

    hop_wait(kv, kv_s, kv_r, 0, range(4))
    hop_send(kv, kv_s, kv_r, 1, range(12))
    local[2].wait()
    arrived(qd.at[theirs, 0:HEAD], sib_s.at[2], sib_r.at[2])
    forward([chip_at(step) for step in GROUPS[0]])

    hop_wait(kv, kv_s, kv_r, 1, range(12))
    hop_send(kv, kv_s, kv_r, 2, range(12))
    arrived(qd.at[theirs, HEAD : 2 * HEAD], sib_s.at[3], sib_r.at[3])
    hop_send(qd, qd_s, qd_r, 0, range(4))
    forward([chip_at(step) for step in GROUPS[1]])

    hop_wait(kv, kv_s, kv_r, 2, range(12))
    hop_send(kv, kv_s, kv_r, 3, range(4))
    hop_wait(qd, qd_s, qd_r, 0, range(4))
    hop_send(qd, qd_s, qd_r, 1, range(12))
    hop_wait(kv, kv_s, kv_r, 3, range(4))
    forward([chip_at(step) for step in GROUPS[2]])

    for a in range(2):
        rs = slice(a * TOK, (a + 1) * TOK)
        denominator = jnp.sum(l[rs, :], axis=1, keepdims=True)
        attention = (acc[rs, :] / denominator).astype(BF16)
        attb[rs, :] = attention
        grads = qd[own_rows(a), HEAD : 2 * HEAD].astype(F32)
        delta = jnp.sum(grads * attention.astype(F32), axis=1, keepdims=True)
        m[rs, :] = jnp.broadcast_to(m[rs, 0:1] + jnp.log2(denominator), (TOK, HEAD))
        l[rs, :] = jnp.broadcast_to(delta, (TOK, HEAD))
    lane = lax.broadcasted_iota(jnp.int32, (CHIP, HEAD), 1)
    st[chip] = jnp.transpose(jnp.where(lane == 0, m[...], l[...]))[0:8, :]

    send(st.at[chip], st.at[chip], st_s.at[0], st_r.at[0], at(RIGHT))
    send(st.at[chip], st.at[chip], st_s.at[1], st_r.at[1], at(LEFT))
    own_att = pltpu.make_async_copy(attb.at[half], ag.at[z, :, cols(c)], loc.at[6])
    own_att.start()
    send(attb.at[other_half], ag.at[z, :, cols(c)], sib_s.at[5], sib_r.at[5], twin)

    arrived(gyc.at[other_half], sib_s.at[4], sib_r.at[4])
    att_t = jnp.transpose(attb[...].astype(F32)).astype(BF16)

    @pl.loop(0, 16)
    def _(n):
        part = dot(att_t, gyc[:, pl.ds(pl.multiple_of(n * 256, 256), 256)])
        gb[n // 4, lax.rem(n, 4)] = part.astype(BF16)

    own_att.wait()
    arrived(ag.at[z, :, cols(o)], sib_s.at[5], sib_r.at[5])

    def z_at(step):
        return wrap(z + step, N_Z)

    def z_hop(n, block, way, part=None):
        place = ag.at[z_at(block)] if part is None else ag.at[z_at(block), part]
        send(place, place, az_s.at[n], az_r.at[n], (s, z_at(way)))

    def z_wait(n, block, part=None):
        place = ag.at[z_at(block)] if part is None else ag.at[z_at(block), part]
        arrived(place, az_s.at[n], az_r.at[n])

    top, low = slice(0, HALF), slice(HALF, TOK)
    z_hop(0, 0, 1)
    z_hop(1, 0, -1)

    upper, lower = slice(0, 64), slice(64, 128)
    for d in (1, 2, 3):
        send(gb.at[:, wrap(x + d, 4), upper], r1.at[0, d - 1], g1_s.at[0, d - 1], g1_r.at[0, d - 1], at((0, d)))
        send(gb.at[wrap(y + d, 4), :, lower], r1.at[1, d - 1], g1_s.at[1, d - 1], g1_r.at[1, d - 1], at((d, 0)))

    def st_row(step):
        return st.at[pl.ds(wrap(y + step, 4) * 4, 4)]

    def st_at(step):
        return st.at[chip_at(step)]

    arrived(st_at((0, -1)), st_s.at[0], st_r.at[0])
    send(st_at((0, -1)), st_at((0, -1)), st_s.at[2], st_r.at[2], at(RIGHT))
    query_grad(list(range(0, 4)))
    arrived(st_at((0, 1)), st_s.at[1], st_r.at[1])
    arrived(st_at((0, 2)), st_s.at[2], st_r.at[2])
    send(st_row(0), st_row(0), st_s.at[3], st_r.at[3], at(DOWN))
    send(st_row(0), st_row(0), st_s.at[4], st_r.at[4], at(UP))
    z_wait(0, -1)
    z_hop(2, -1, 1)
    z_wait(1, 1)
    z_hop(3, 1, -1)
    query_grad(list(range(4, 8)))
    for d in range(1, N_Z):
        place = wc.at[z_at(-d), cols(c)]
        arrived(place, wz_s.at[d - 1], wz_r.at[d - 1])
        send(place, place, ws_s.at[d - 1], ws_r.at[d - 1], twin)
    hop_wait(qd, qd_s, qd_r, 1, range(12))
    hop_send(qd, qd_s, qd_r, 2, range(12))
    arrived(st_row(-1), st_s.at[3], st_r.at[3])
    send(st_row(-1), st_row(-1), st_s.at[5], st_r.at[5], at(DOWN))
    z_wait(2, -2)
    z_hop(4, -2, 1)
    z_wait(3, 2)
    z_hop(5, 2, -1)
    query_grad(list(range(8, 12)))
    arrived(st_row(1), st_s.at[4], st_r.at[4])
    arrived(st_row(2), st_s.at[5], st_r.at[5])
    query_grad(list(range(12, 16)))

    for way in range(2):
        for d in (1, 2, 3):
            arrived(r1.at[way, d - 1], g1_s.at[way, d - 1], g1_r.at[way, d - 1])
    for n in range(4):
        total = gb[n, x, upper].astype(F32)
        for d in range(3):
            total = total + r1[0, d, n].astype(F32)
        h1[0, n] = total.astype(BF16)
        total = gb[y, n, lower].astype(F32)
        for d in range(3):
            total = total + r1[1, d, n].astype(F32)
        h1[1, n] = total.astype(BF16)
    for d in (1, 2, 3):
        send(h1.at[0, wrap(y + d, 4)], r2.at[0, d - 1], g2_s.at[0, d - 1], g2_r.at[0, d - 1], at((d, 0)))
        send(h1.at[1, wrap(x + d, 4)], r2.at[1, d - 1], g2_s.at[1, d - 1], g2_r.at[1, d - 1], at((0, d)))

    key_grad([chip_at(step) for step in GROUPS[0]])
    z_wait(4, -3)
    z_hop(6, -3, 1, top)
    z_wait(5, 3)
    z_hop(7, 3, -1, low)
    key_grad([chip_at(step) for step in GROUPS[1]])
    hop_wait(qd, qd_s, qd_r, 2, range(12))
    hop_send(qd, qd_s, qd_r, 3, range(4))

    for way in range(2):
        for d in (1, 2, 3):
            arrived(r2.at[way, d - 1], g2_s.at[way, d - 1], g2_r.at[way, d - 1])
    for way, own in ((0, y), (1, x)):
        total = h1[way, own].astype(F32)
        for d in range(3):
            total = total + r2[way, d].astype(F32)
        total = total.astype(BF16)
        rs = slice(way * 64, way * 64 + 64)
        gf[0, rs, :] = jnp.where(c == 0, total[:, 0:HEAD], total[:, HEAD:])
        gf[1, rs, :] = jnp.where(c == 0, total[:, HEAD:], total[:, 0:HEAD])
    send(gf.at[1], gswap, sib_s.at[6], sib_r.at[6], twin)

    for d in range(1, N_Z):
        arrived(wc.at[z_at(-d), cols(o)], ws_s.at[d - 1], ws_r.at[d - 1])
    z_wait(6, -4, top)
    z_wait(7, 4, low)
    local[5].wait()
    total = dot(ag[0], wc[0])
    for n in range(1, N_Z):
        total = total + dot(ag[n], wc[n])
    out_ref[...] = total.astype(BF16)

    hop_wait(qd, qd_s, qd_r, 3, range(4))
    key_grad([chip_at(step) for step in GROUPS[2]])

    for n, (ref, factor) in enumerate(((dq, SCALE), (dk, SCALE), (dv, 1.0))):
        swap[0, n] = (ref[...] * factor).astype(BF16)
        send(swap.at[0, n, other_half], swap.at[1, n, 0:TOK], sib_s.at[7 + n], sib_r.at[7 + n], twin)
    arrived(gswap, sib_s.at[6], sib_r.at[6])
    gw_ref[0:HEAD, :] = jnp.where(c == 0, gf[0], gswap[...])
    gw_ref[HEAD : 2 * HEAD, :] = jnp.where(c == 0, gswap[...], gf[0])
    for n, ref in enumerate((dq_ref, dk_ref, dv_ref)):
        arrived(swap.at[1, n, 0:TOK], sib_s.at[7 + n], sib_r.at[7 + n])
        own = swap[0, n, half, :]
        other = swap[1, n, 0:TOK, :]
        ref[:, 0:HEAD] = jnp.where(c == 0, own, other)
        ref[:, HEAD : 2 * HEAD] = jnp.where(c == 0, other, own)
    for copy in sent:
        copy.wait_send()


def shards(queries, key_states, value_states, w_out, grad_y, chain_order):
    anywhere = pl.BlockSpec(memory_space=pl.ANY)
    vmem = pl.BlockSpec(memory_space=pltpu.VMEM)
    dma = pltpu.SemaphoreType.DMA
    tokens = 32 * TOK
    tile = jax.ShapeDtypeStruct((TOK, 2 * HEAD), BF16)
    scratch = [
        pltpu.VMEM((tokens, 2 * HEAD), BF16),
        pltpu.VMEM((tokens, 2 * HEAD), BF16),
        pltpu.VMEM((2 * HEAD, 4096), BF16),
        pltpu.VMEM((CHIP, 4096), BF16),
        pltpu.VMEM((N_Z, 2 * HEAD, 512), BF16),
        pltpu.VMEM((N_Z, TOK, 2 * HEAD), BF16),
        pltpu.VMEM((4, 4, HEAD, 256), BF16),
        pltpu.VMEM((2, 3, 4, 64, 256), BF16),
        pltpu.VMEM((2, 4, 64, 256), BF16),
        pltpu.VMEM((2, 3, 64, 256), BF16),
        pltpu.VMEM((2, HEAD, HEAD), BF16),
        pltpu.VMEM((16, 8, CHIP), F32),
        pltpu.VMEM((CHIP, HEAD), BF16),
        pltpu.VMEM((2, TOK, HEAD), BF16),
        pltpu.VMEM((2, 3, CHIP, HEAD), BF16),
        pltpu.VMEM((HEAD, HEAD), BF16),
    ]
    scratch += [pltpu.VMEM((CHIP, HEAD), F32)] * 6
    scratch += [dma((N_COPIES,))] * 4
    scratch += [dma((7,)), dma((10,)), dma((10,))]
    scratch += [dma((7,))] * 4
    scratch += [dma((6,))] * 2
    scratch += [dma((8,))] * 2
    scratch += [dma((2, 3))] * 4
    return pl.pallas_call(
        kernel,
        out_shape=(
            jax.ShapeDtypeStruct((TOK, 512), BF16),
            tile,
            tile,
            tile,
            jax.ShapeDtypeStruct((2 * HEAD, HEAD), BF16),
        ),
        in_specs=[anywhere] * 5 + [pl.BlockSpec(memory_space=pltpu.SMEM)],
        out_specs=(vmem,) * 5,
        scratch_shapes=scratch,
        compiler_params=pltpu.CompilerParams(
            collective_id=0, has_side_effects=True, vmem_limit_bytes=56 * 1024 * 1024
        ),
        name="attention_layer",
    )(queries, key_states, value_states, w_out, grad_y, chain_order)


def solution(mesh):
    return jax.shard_map(
        shards,
        mesh=mesh,
        in_specs=(
            P("seq", "head"),
            P("seq", "head"),
            P("seq", "head"),
            P("head", None),
            P("seq", None),
            P(),
        ),
        out_specs=(
            P("seq", "head"),
            P("seq", "head"),
            P("seq", "head"),
            P("seq", "head"),
            P("head", "seq"),
        ),
        check_vma=False,
    )
```

```python
import math

import jax
import jax.numpy as jnp
from jax import lax
from jax.experimental import pallas as pl
from jax.experimental.pallas import tpu as pltpu
from jax.sharding import PartitionSpec as P

F32 = jnp.float32
BF16 = jnp.bfloat16
MESH = pl.DeviceIdType.MESH
HEAD = 128
TOK = 192
CHIP = 2 * TOK
HALF = TOK // 2
N_Z = 8
SCALE = 1.0 / math.sqrt(HEAD)
SCALE2 = SCALE * math.log2(math.e)
NEG = -1e30

RIGHT, LEFT, DOWN, UP = (0, 1), (0, -1), (1, 0), (-1, 0)
EVEN, ODD = (0, TOK), (TOK, TOK)
EVEN_TOP, EVEN_LOW = (0, HALF), (HALF, HALF)
ODD_TOP, ODD_LOW = (TOK, HALF), (TOK + HALF, HALF)
WHOLE = (0, CHIP)

FLOWS = [
    [
        [((0, 0), EVEN, d) for d in (RIGHT, LEFT, DOWN, UP)],
        [
            ((0, -1), EVEN, DOWN),
            ((0, -1), EVEN, UP),
            ((0, -1), EVEN, RIGHT),
            ((0, 1), EVEN, DOWN),
            ((0, 1), EVEN, UP),
            ((-1, 0), EVEN, DOWN),
        ],
        [
            ((0, 2), EVEN, DOWN),
            ((0, 2), EVEN, UP),
            ((-1, -1), EVEN_TOP, DOWN),
            ((-1, 1), EVEN_TOP, DOWN),
            ((1, -1), EVEN_LOW, UP),
            ((1, 1), EVEN_LOW, UP),
        ],
        [((-1, 2), EVEN_TOP, DOWN), ((1, 2), EVEN_LOW, UP)],
    ],
    [
        [((0, 0), ODD, d) for d in (RIGHT, LEFT, DOWN, UP)],
        [
            ((1, 0), ODD, RIGHT),
            ((1, 0), ODD, LEFT),
            ((1, 0), ODD, UP),
            ((-1, 0), ODD, RIGHT),
            ((-1, 0), ODD, LEFT),
            ((0, 1), ODD, LEFT),
        ],
        [
            ((2, 0), ODD, RIGHT),
            ((2, 0), ODD, LEFT),
            ((-1, -1), ODD_TOP, RIGHT),
            ((1, -1), ODD_TOP, RIGHT),
            ((-1, 1), ODD_LOW, LEFT),
            ((1, 1), ODD_LOW, LEFT),
        ],
        [((2, -1), ODD_TOP, RIGHT), ((2, 1), ODD_LOW, LEFT)],
    ],
]
FIRST = [0, 4, 10, 16]
N_COPIES = 18
GROUPS = [
    [(0, 0), (0, -1), (0, 1), (-1, 0), (1, 0)],
    [(0, 2), (2, 0), (-1, -1), (-1, 1), (1, -1), (1, 1)],
    [(-1, 2), (1, 2), (2, -1), (2, 1), (2, 2)],
]


def dot(a, b):
    return jnp.dot(a, b, preferred_element_type=F32)


def dot_nt(a, b):
    return lax.dot_general(a, b, (((1,), (1,)), ((), ())), preferred_element_type=F32)


def wrap(value, size):
    return lax.rem(value + 2 * size, size)


def kernel(
    q_hbm, k_hbm, v_hbm, w_hbm, gy_hbm, order,
    out_ref, dq_ref, dk_ref, dv_ref, gw_ref,
    kv, qd, wv, gyc, wc, ag, gb, r1, h1, r2, gf, st, attb, kvs, qds, swap, gswap,
    m, l, acc, dq, dk, dv,
    kv_s, kv_r, qd_s, qd_r, own_s, own_r, loc, sib_s, sib_r, wz_s, wz_r, ws_s, ws_r, st_s, st_r,
    az_s, az_r, a0_s, a0_r, g1_s, g1_r, g2_s, g2_r,
):
    s = lax.axis_index("seq")
    z = lax.axis_index("head")
    y = s // 8
    x = lax.rem(s // 2, 4)
    c = lax.rem(s, 2)
    chip = y * 4 + x
    twin = (s + 1 - 2 * c, z)
    o = 1 - c

    def at(step):
        return ((wrap(y + step[0], 4) * 4 + wrap(x + step[1], 4)) * 2 + c, z)

    def chip_at(step):
        return wrap(y + step[0], 4) * 4 + wrap(x + step[1], 4)

    def rows(step, part=WHOLE):
        return pl.ds(pl.multiple_of(chip_at(step) * CHIP + part[0], 32), part[1])

    def cols(index, size=HEAD):
        return pl.ds(pl.multiple_of(index * size, size), size)

    def remote(src, dst, send, recv, device):
        return pltpu.make_async_remote_copy(
            src_ref=src, dst_ref=dst, send_sem=send, recv_sem=recv, device_id=device, device_id_type=MESH
        )

    sent = []

    def send(src, dst, ssem, rsem, device):
        copy = remote(src, dst, ssem, rsem, device)
        copy.start()
        sent.append(copy)

    def arrived(dst, ssem, rsem):
        remote(dst, dst, ssem, rsem, twin).wait_recv()

    def same(a, b):
        return (a[0] - b[0]) % 4 == 0 and (a[1] - b[1]) % 4 == 0

    def hop_send(buf, ssem, rsem, flow, hop, step=None):
        for i, (source, part, way) in enumerate(FLOWS[flow][hop]):
            if step is None or same(step, source):
                place = buf.at[rows(source, part)]
                n = FIRST[hop] + i
                send(place, place, ssem.at[flow, n], rsem.at[flow, n], at(way))

    def relay(buf, ssem, rsem, flow, hop):
        for i, (source, part, way) in enumerate(FLOWS[flow][hop]):
            step = (source[0] - way[0], source[1] - way[1])
            n = FIRST[hop] + i
            arrived(buf.at[rows(step, part)], ssem.at[flow, n], rsem.at[flow, n])
            if hop < 3:
                hop_send(buf, ssem, rsem, flow, hop + 1, step)

    mine = pl.ds(pl.multiple_of(s * TOK, 32), TOK)
    half = pl.ds(pl.multiple_of(c * TOK, 32), TOK)
    other_half = pl.ds(pl.multiple_of(o * TOK, 32), TOK)
    local = []
    for h in range(2):
        local += [
            pltpu.make_async_copy(k_hbm.at[:, cols(h)], kvs.at[h, :, 0:HEAD], loc.at[3 * h]),
            pltpu.make_async_copy(v_hbm.at[:, cols(h)], kvs.at[h, :, HEAD : 2 * HEAD], loc.at[3 * h + 1]),
            pltpu.make_async_copy(q_hbm.at[:, cols(h)], qds.at[h, :, 0:HEAD], loc.at[3 * h + 2]),
        ]
    local += [
        pltpu.make_async_copy(w_hbm, wv, loc.at[6]),
        pltpu.make_async_copy(gy_hbm, gyc.at[half], loc.at[7]),
        pltpu.make_async_copy(w_hbm.at[:, cols(z, 512)], wc.at[z], loc.at[8]),
    ]
    for copy in local:
        copy.start()
    m[...] = jnp.full_like(m, NEG)
    for ref in (l, acc, dq, dk, dv):
        ref[...] = jnp.zeros_like(ref)

    barrier = pltpu.get_barrier_semaphore()
    peers = [twin, (twin[0], wrap(z + 1, N_Z)), (twin[0], wrap(z - 1, N_Z))]
    for way in (RIGHT, LEFT, DOWN, UP):
        peers.append((chip_at(way) * 2 + o, z))
    for d in (1, 2, 3):
        peers += [at((0, d)), at((d, 0))]
    for d in range(1, N_Z):
        peers.append((s, wrap(z + d, N_Z)))
    for peer in peers:
        pl.semaphore_signal(barrier, inc=1, device_id=peer, device_id_type=MESH)
    pl.semaphore_wait(barrier, len(peers))

    def first_send(buf, stage, which, ssem, rsem):
        for i, way in enumerate((RIGHT, LEFT, DOWN, UP)):
            for h in range(2):
                send(stage.at[h], buf.at[mine], ssem.at[h, i], rsem.at[c, i], (chip_at(way) * 2 + h, z))
        send(stage.at[o], buf.at[mine], own_s.at[which], own_r.at[which], twin)
        own = pltpu.make_async_copy(stage.at[c], buf.at[mine], loc.at[9 + which])
        own.start()
        return own

    theirs = pl.ds(pl.multiple_of((s + 1 - 2 * c) * TOK, 32), TOK)
    for n in (0, 1, 3, 4):
        local[n].wait()
    own_kv = first_send(kv, kvs, 0, kv_s, kv_r)
    for d in range(1, N_Z):
        far = wrap(z + d, N_Z)
        send(
            w_hbm.at[cols(c), cols(far, 512)], wc.at[z, cols(c)], wz_s.at[d - 1], wz_r.at[d - 1], (s, far)
        )
    send(gy_hbm, gyc.at[half], sib_s.at[4], sib_r.at[4], twin)

    local[6].wait()
    local[7].wait()
    d_own = dot_nt(gyc[half, :], wv[...]).astype(BF16)
    qds[0, :, HEAD : 2 * HEAD] = d_own[:, 0:HEAD]
    qds[1, :, HEAD : 2 * HEAD] = d_own[:, HEAD:]
    local[2].wait()
    local[5].wait()

    def block_pos(index):
        return order[index] * TOK

    def row_pos(chips):
        lane = lax.broadcasted_iota(jnp.int32, (1, CHIP), 1)
        parts = [
            jnp.where(lane < TOK, block_pos(2 * n), block_pos(2 * n + 1) - TOK) + lane for n in chips
        ]
        return jnp.concatenate(parts, axis=1)

    def col_pos(a):
        return lax.broadcasted_iota(jnp.int32, (TOK, 1), 0) + block_pos(2 * chip + a)

    def own_rows(a):
        return pl.ds(pl.multiple_of(chip * CHIP + a * TOK, 32), TOK)

    def chip_rows(n):
        return pl.ds(pl.multiple_of(n * CHIP, 128), CHIP)

    def forward(chips):
        keys = jnp.concatenate([kv[chip_rows(n), 0:HEAD] for n in chips], axis=0)
        values = jnp.concatenate([kv[chip_rows(n), HEAD : 2 * HEAD] for n in chips], axis=0)
        key_pos = row_pos(chips)
        for a in range(2):
            rs = slice(a * TOK, (a + 1) * TOK)
            scores = dot_nt(qd[own_rows(a), 0:HEAD], keys) * SCALE2
            scores = jnp.where(key_pos <= col_pos(a), scores, NEG)
            before = m[rs, 0:1]
            now = jnp.maximum(before, jnp.max(scores, axis=1, keepdims=True))
            factor = jnp.exp2(before - now)
            weights = jnp.exp2(scores - now)
            m[rs, :] = jnp.broadcast_to(now, (TOK, HEAD))
            total = weights[:, 0:HEAD]
            for t in range(1, weights.shape[1] // HEAD):
                total = total + weights[:, t * HEAD : (t + 1) * HEAD]
            l[rs, :] = l[rs, :] * factor + total
            acc[rs, :] = acc[rs, :] * factor + dot(weights.astype(BF16), values)

    def query_grad(chips):
        keys = jnp.concatenate([kv[chip_rows(n), 0:HEAD] for n in chips], axis=0)
        values = jnp.concatenate([kv[chip_rows(n), HEAD : 2 * HEAD] for n in chips], axis=0)
        key_pos = row_pos(chips)
        for a in range(2):
            rs = slice(a * TOK, (a + 1) * TOK)
            scores = dot_nt(qd[own_rows(a), 0:HEAD], keys) * SCALE2 - m[rs, 0:1]
            probs = jnp.exp2(jnp.where(key_pos <= col_pos(a), scores, NEG))
            slopes = dot_nt(qd[own_rows(a), HEAD : 2 * HEAD], values)
            dscore = (probs * (slopes - l[rs, 0:1])).astype(BF16)
            dq[rs, :] += dot(dscore, keys)

    def key_grad(chips):
        queries = jnp.concatenate([qd[chip_rows(n), 0:HEAD] for n in chips], axis=0)
        douts = jnp.concatenate([qd[chip_rows(n), HEAD : 2 * HEAD] for n in chips], axis=0)
        query_pos = row_pos(chips)
        norm = jnp.concatenate([st[n, 0:1, :] for n in chips], axis=1)
        delta = jnp.concatenate([st[n, 1:2, :] for n in chips], axis=1)
        for a in range(2):
            rs = slice(a * TOK, (a + 1) * TOK)
            scores = dot_nt(kv[own_rows(a), 0:HEAD], queries) * SCALE2 - norm
            probs = jnp.exp2(jnp.where(col_pos(a) <= query_pos, scores, NEG))
            dv[rs, :] += dot(probs.astype(BF16), douts)
            slopes = dot_nt(kv[own_rows(a), HEAD : 2 * HEAD], douts)
            dscore = (probs * (slopes - delta)).astype(BF16)
            dk[rs, :] += dot(dscore, queries)

    relay(kv, kv_s, kv_r, 0, 0)
    relay(kv, kv_s, kv_r, 1, 0)
    own_kv.wait()
    arrived(kv.at[theirs], own_s.at[0], own_r.at[0])
    own_qd = first_send(qd, qds, 1, qd_s, qd_r)
    own_qd.wait()
    arrived(qd.at[theirs], own_s.at[1], own_r.at[1])
    forward([chip_at(step) for step in GROUPS[0]])

    relay(kv, kv_s, kv_r, 0, 1)
    relay(kv, kv_s, kv_r, 1, 1)
    forward([chip_at(step) for step in GROUPS[1]])

    relay(kv, kv_s, kv_r, 0, 2)
    relay(kv, kv_s, kv_r, 1, 2)
    relay(qd, qd_s, qd_r, 0, 0)
    relay(qd, qd_s, qd_r, 1, 0)
    forward([chip_at(step) for step in GROUPS[2][:4]])
    relay(kv, kv_s, kv_r, 0, 3)
    relay(kv, kv_s, kv_r, 1, 3)
    forward([chip_at(step) for step in GROUPS[2][4:]])

    for a in range(2):
        rs = slice(a * TOK, (a + 1) * TOK)
        denominator = jnp.sum(l[rs, :], axis=1, keepdims=True)
        attention = (acc[rs, :] / denominator).astype(BF16)
        attb[rs, :] = attention
        grads = qd[own_rows(a), HEAD : 2 * HEAD].astype(F32)
        delta = jnp.sum(grads * attention.astype(F32), axis=1, keepdims=True)
        m[rs, :] = jnp.broadcast_to(m[rs, 0:1] + jnp.log2(denominator), (TOK, HEAD))
        l[rs, :] = jnp.broadcast_to(delta, (TOK, HEAD))
    lane = lax.broadcasted_iota(jnp.int32, (CHIP, HEAD), 1)
    st[chip] = jnp.transpose(jnp.where(lane == 0, m[...], l[...]))[0:8, :]

    for d in (1, 2, 3):
        send(st.at[chip], st.at[chip], st_s.at[0, d - 1], st_r.at[0, d - 1], at((0, d)))
    own_att = pltpu.make_async_copy(attb.at[half], ag.at[z, :, cols(c)], loc.at[11])
    own_att.start()
    for part in range(2):
        for n, step in enumerate((1, -1)):
            for h in range(2):
                send(
                    attb.at[h * TOK + part * HALF : h * TOK + (part + 1) * HALF],
                    ag.at[z, part * HALF : (part + 1) * HALF, cols(c)],
                    a0_s.at[2 * n + part, h],
                    a0_r.at[2 * n + part, c],
                    (chip * 2 + h, wrap(z + step, N_Z)),
                )
    send(attb.at[other_half], ag.at[z, :, cols(c)], sib_s.at[5], sib_r.at[5], twin)

    arrived(gyc.at[other_half], sib_s.at[4], sib_r.at[4])
    att_t = jnp.transpose(attb[...].astype(F32)).astype(BF16)

    @pl.loop(0, 16)
    def _(n):
        part = dot(att_t, gyc[:, pl.ds(pl.multiple_of(n * 256, 256), 256)])
        gb[n // 4, lax.rem(n, 4)] = part.astype(BF16)


    def z_at(step):
        return wrap(z + step, N_Z)

    def z_place(block, part):
        return ag.at[z_at(block), part * HALF : (part + 1) * HALF]

    def z_send(hop, way, part):
        place = z_place(-way * hop, part)
        n = way_index(way), 2 * hop + part
        send(place, place, az_s.at[n], az_r.at[n], (s, z_at(way)))

    def way_index(way):
        return 0 if way > 0 else 1

    def z_relay(hop):
        for part in (0, 1):
            for way in (1, -1):
                if hop == 3 and part != way_index(way):
                    continue
                n = way_index(way), 2 * hop + part
                if hop == 0:
                    for h in range(2):
                        place = ag.at[z_at(-way), part * HALF : (part + 1) * HALF, cols(h)]
                        arrived(place, a0_s.at[2 * n[0] + part, h], a0_r.at[2 * n[0] + part, h])
                else:
                    arrived(z_place(-way * (hop + 1), part), az_s.at[n], az_r.at[n])
                if hop < 2 or (hop == 2 and part == way_index(way)):
                    z_send(hop + 1, way, part)

    upper, lower = slice(0, 64), slice(64, 128)
    for d in (1, 2, 3):
        send(gb.at[:, wrap(x + d, 4), upper], r1.at[0, d - 1], g1_s.at[0, d - 1], g1_r.at[0, d - 1], at((0, d)))
        send(gb.at[wrap(y + d, 4), :, lower], r1.at[1, d - 1], g1_s.at[1, d - 1], g1_r.at[1, d - 1], at((d, 0)))

    def st_row(step):
        return st.at[pl.ds(wrap(y + step, 4) * 4, 4)]

    def swap_send(n, ref, factor):
        swap[0, n] = (ref[...] * factor).astype(BF16)
        send(swap.at[0, n, other_half], swap.at[1, n, 0:TOK], sib_s.at[7 + n], sib_r.at[7 + n], twin)

    relay(qd, qd_s, qd_r, 0, 1)
    relay(qd, qd_s, qd_r, 1, 1)
    z_relay(0)
    for d in (1, 2, 3):
        arrived(st.at[chip_at((0, -d))], st_s.at[0, d - 1], st_r.at[0, d - 1])
    for d in (1, 2, 3):
        send(st_row(0), st_row(0), st_s.at[1, d - 1], st_r.at[1, d - 1], at((d, 0)))
    query_grad(list(range(0, 4)))
    query_grad(list(range(4, 8)))
    z_relay(1)
    for d in range(1, N_Z):
        place = wc.at[z_at(-d), cols(c)]
        arrived(place, wz_s.at[d - 1], wz_r.at[d - 1])
        send(place, place, ws_s.at[d - 1], ws_r.at[d - 1], twin)
    query_grad(list(range(8, 12)))
    relay(qd, qd_s, qd_r, 0, 2)
    relay(qd, qd_s, qd_r, 1, 2)
    z_relay(2)
    query_grad(list(range(12, 16)))
    for d in (1, 2, 3):
        arrived(st_row(-d), st_s.at[1, d - 1], st_r.at[1, d - 1])
    swap_send(0, dq, SCALE)

    for way in range(2):
        for d in (1, 2, 3):
            arrived(r1.at[way, d - 1], g1_s.at[way, d - 1], g1_r.at[way, d - 1])
    for n in range(4):
        total = gb[n, x, upper].astype(F32)
        for d in range(3):
            total = total + r1[0, d, n].astype(F32)
        h1[0, n] = total.astype(BF16)
        total = gb[y, n, lower].astype(F32)
        for d in range(3):
            total = total + r1[1, d, n].astype(F32)
        h1[1, n] = total.astype(BF16)
    for d in (1, 2, 3):
        send(h1.at[0, wrap(y + d, 4)], r2.at[0, d - 1], g2_s.at[0, d - 1], g2_r.at[0, d - 1], at((d, 0)))
        send(h1.at[1, wrap(x + d, 4)], r2.at[1, d - 1], g2_s.at[1, d - 1], g2_r.at[1, d - 1], at((0, d)))

    key_grad([chip_at(step) for step in GROUPS[0]])
    key_grad([chip_at(step) for step in GROUPS[1]])

    for way in range(2):
        for d in (1, 2, 3):
            arrived(r2.at[way, d - 1], g2_s.at[way, d - 1], g2_r.at[way, d - 1])
    for way, own in ((0, y), (1, x)):
        total = h1[way, own].astype(F32)
        for d in range(3):
            total = total + r2[way, d].astype(F32)
        total = total.astype(BF16)
        rs = slice(way * 64, way * 64 + 64)
        gf[0, rs, :] = jnp.where(c == 0, total[:, 0:HEAD], total[:, HEAD:])
        gf[1, rs, :] = jnp.where(c == 0, total[:, HEAD:], total[:, 0:HEAD])
    send(gf.at[1], gswap, sib_s.at[6], sib_r.at[6], twin)

    for d in range(1, N_Z):
        arrived(wc.at[z_at(-d), cols(o)], ws_s.at[d - 1], ws_r.at[d - 1])
    z_relay(3)
    local[8].wait()
    own_att.wait()
    arrived(ag.at[z, :, cols(o)], sib_s.at[5], sib_r.at[5])
    total = dot(ag[0], wc[0])
    for n in range(1, N_Z):
        total = total + dot(ag[n], wc[n])
    out_ref[...] = total.astype(BF16)

    relay(qd, qd_s, qd_r, 0, 3)
    relay(qd, qd_s, qd_r, 1, 3)
    key_grad([chip_at(step) for step in GROUPS[2]])

    swap_send(1, dk, SCALE)
    swap_send(2, dv, 1.0)
    arrived(gswap, sib_s.at[6], sib_r.at[6])
    gw_ref[0:HEAD, :] = jnp.where(c == 0, gf[0], gswap[...])
    gw_ref[HEAD : 2 * HEAD, :] = jnp.where(c == 0, gswap[...], gf[0])
    for n, ref in enumerate((dq_ref, dk_ref, dv_ref)):
        arrived(swap.at[1, n, 0:TOK], sib_s.at[7 + n], sib_r.at[7 + n])
        own = swap[0, n, half, :]
        other = swap[1, n, 0:TOK, :]
        ref[:, 0:HEAD] = jnp.where(c == 0, own, other)
        ref[:, HEAD : 2 * HEAD] = jnp.where(c == 0, other, own)
    for copy in sent:
        copy.wait_send()


def copy_kernel(*refs):
    for n in range(5):
        refs[5 + n][...] = refs[n][...]


def shards(queries, key_states, value_states, w_out, grad_y, chain_order):
    anywhere = pl.BlockSpec(memory_space=pl.ANY)
    vmem = pl.BlockSpec(memory_space=pltpu.VMEM)
    dma = pltpu.SemaphoreType.DMA
    tokens = 32 * TOK
    tile = jax.ShapeDtypeStruct((TOK, 2 * HEAD), BF16)
    scratch = [
        pltpu.VMEM((tokens, 2 * HEAD), BF16),
        pltpu.VMEM((tokens, 2 * HEAD), BF16),
        pltpu.VMEM((2 * HEAD, 4096), BF16),
        pltpu.VMEM((CHIP, 4096), BF16),
        pltpu.VMEM((N_Z, 2 * HEAD, 512), BF16),
        pltpu.VMEM((N_Z, TOK, 2 * HEAD), BF16),
        pltpu.VMEM((4, 4, HEAD, 256), BF16),
        pltpu.VMEM((2, 3, 4, 64, 256), BF16),
        pltpu.VMEM((2, 4, 64, 256), BF16),
        pltpu.VMEM((2, 3, 64, 256), BF16),
        pltpu.VMEM((2, HEAD, HEAD), BF16),
        pltpu.VMEM((16, 8, CHIP), F32),
        pltpu.VMEM((CHIP, HEAD), BF16),
        pltpu.VMEM((2, TOK, 2 * HEAD), BF16),
        pltpu.VMEM((2, TOK, 2 * HEAD), BF16),
        pltpu.VMEM((2, 3, CHIP, HEAD), BF16),
        pltpu.VMEM((HEAD, HEAD), BF16),
    ]
    scratch += [pltpu.VMEM((CHIP, HEAD), F32)] * 6
    scratch += [dma((2, N_COPIES))] * 4
    scratch += [dma((2,)), dma((2,)), dma((12,)), dma((10,)), dma((10,))]
    scratch += [dma((7,))] * 4
    scratch += [dma((2, 3))] * 2
    scratch += [dma((2, 8))] * 2
    scratch += [dma((4, 2))] * 2
    scratch += [dma((2, 3))] * 4
    results = pl.pallas_call(
        kernel,
        out_shape=(
            jax.ShapeDtypeStruct((TOK, 512), BF16),
            tile,
            tile,
            tile,
            jax.ShapeDtypeStruct((2 * HEAD, HEAD), BF16),
        ),
        in_specs=[anywhere] * 5 + [pl.BlockSpec(memory_space=pltpu.SMEM)],
        out_specs=(vmem,) * 5,
        scratch_shapes=scratch,
        compiler_params=pltpu.CompilerParams(
            collective_id=0, has_side_effects=True, vmem_limit_bytes=56 * 1024 * 1024
        ),
        name="attention_layer",
    )(queries, key_states, value_states, w_out, grad_y, chain_order)
    return pl.pallas_call(
        copy_kernel,
        out_shape=tuple(jax.ShapeDtypeStruct(r.shape, r.dtype) for r in results),
        in_specs=[vmem] * 5,
        out_specs=(vmem,) * 5,
        name="results",
    )(*results)


def solution(mesh):
    return jax.shard_map(
        shards,
        mesh=mesh,
        in_specs=(
            P("seq", "head"),
            P("seq", "head"),
            P("seq", "head"),
            P("head", None),
            P("seq", None),
            P(),
        ),
        out_specs=(
            P("seq", "head"),
            P("seq", "head"),
            P("seq", "head"),
            P("seq", "head"),
            P("head", "seq"),
        ),
        check_vma=False,
    )
```

```python
import math

import jax
import jax.numpy as jnp
from jax import lax
from jax.experimental import pallas as pl
from jax.experimental.pallas import tpu as pltpu
from jax.sharding import PartitionSpec as P

F32 = jnp.float32
BF16 = jnp.bfloat16
MESH = pl.DeviceIdType.MESH
HEAD = 128
TOK = 192
CHIP = 2 * TOK
HALF = TOK // 2
N_Z = 8
SCALE = 1.0 / math.sqrt(HEAD)
SCALE2 = SCALE * math.log2(math.e)
NEG = -1e30

RIGHT, LEFT, DOWN, UP = (0, 1), (0, -1), (1, 0), (-1, 0)
EVEN, ODD = (0, TOK), (TOK, TOK)
EVEN_TOP, EVEN_LOW = (0, HALF), (HALF, HALF)
ODD_TOP, ODD_LOW = (TOK, HALF), (TOK + HALF, HALF)
WHOLE = (0, CHIP)

FLOWS = [
    [
        [((0, 0), EVEN, d) for d in (RIGHT, LEFT, DOWN, UP)],
        [
            ((0, -1), EVEN, DOWN),
            ((0, -1), EVEN, UP),
            ((0, -1), EVEN, RIGHT),
            ((0, 1), EVEN, DOWN),
            ((0, 1), EVEN, UP),
            ((-1, 0), EVEN, DOWN),
        ],
        [
            ((0, 2), EVEN, DOWN),
            ((0, 2), EVEN, UP),
            ((-1, -1), EVEN_TOP, DOWN),
            ((-1, 1), EVEN_TOP, DOWN),
            ((1, -1), EVEN_LOW, UP),
            ((1, 1), EVEN_LOW, UP),
        ],
        [((-1, 2), EVEN_TOP, DOWN), ((1, 2), EVEN_LOW, UP)],
    ],
    [
        [((0, 0), ODD, d) for d in (RIGHT, LEFT, DOWN, UP)],
        [
            ((1, 0), ODD, RIGHT),
            ((1, 0), ODD, LEFT),
            ((1, 0), ODD, UP),
            ((-1, 0), ODD, RIGHT),
            ((-1, 0), ODD, LEFT),
            ((0, 1), ODD, LEFT),
        ],
        [
            ((2, 0), ODD, RIGHT),
            ((2, 0), ODD, LEFT),
            ((-1, -1), ODD_TOP, RIGHT),
            ((1, -1), ODD_TOP, RIGHT),
            ((-1, 1), ODD_LOW, LEFT),
            ((1, 1), ODD_LOW, LEFT),
        ],
        [((2, -1), ODD_TOP, RIGHT), ((2, 1), ODD_LOW, LEFT)],
    ],
]
FIRST = [0, 4, 10, 16]
N_COPIES = 18
KV_SENT, QD_SENT, W_SENT, Z_SENT, TWIN_SENT, G_SENT, ST_SENT = range(7)
N_GROUPS = 7
GROUPS = [
    [(0, 0), (0, -1), (0, 1), (-1, 0), (1, 0)],
    [(0, 2), (2, 0), (-1, -1), (-1, 1), (1, -1), (1, 1)],
    [(-1, 2), (1, 2), (2, -1), (2, 1), (2, 2)],
]


def dot(a, b):
    return jnp.dot(a, b, preferred_element_type=F32)


def dot_nt(a, b):
    return lax.dot_general(a, b, (((1,), (1,)), ((), ())), preferred_element_type=F32)


def wrap(value, size):
    return lax.rem(value + 2 * size, size)


def kernel(
    q_hbm, k_hbm, v_hbm, w_hbm, gy_hbm, order,
    out_ref, dq_ref, dk_ref, dv_ref, gw_ref,
    kv, qd, wv, gyc, wc, ag, gb, ga, gt, gr, h1, ga2, gt2, gr2, st, attb, kvs, qds, swap, gswap,
    m, l, acc, dq, dk, dv,
    out_s, kv_r, qd_r, own_r, loc, sib_r, wz_r, ws_r, st_r, az_r, a0_r, g_r, gw_r,
):
    s = lax.axis_index("seq")
    z = lax.axis_index("head")
    y = s // 8
    x = lax.rem(s // 2, 4)
    c = lax.rem(s, 2)
    chip = y * 4 + x
    twin = (s + 1 - 2 * c, z)
    o = 1 - c

    def at(step):
        return ((wrap(y + step[0], 4) * 4 + wrap(x + step[1], 4)) * 2 + c, z)

    def chip_at(step):
        return wrap(y + step[0], 4) * 4 + wrap(x + step[1], 4)

    def rows(step, part=WHOLE):
        return pl.ds(pl.multiple_of(chip_at(step) * CHIP + part[0], 32), part[1])

    def cols(index, size=HEAD):
        return pl.ds(pl.multiple_of(index * size, size), size)

    def remote(src, dst, send, recv, device):
        return pltpu.make_async_remote_copy(
            src_ref=src, dst_ref=dst, send_sem=send, recv_sem=recv, device_id=device, device_id_type=MESH
        )

    totals = [0] * N_GROUPS

    def send(src, dst, group, rsem, device):
        remote(src, dst, out_s.at[group], rsem, device).start()
        totals[group] += math.prod(src.shape)

    def all_sent():
        for group, total in enumerate(totals):
            if group == ST_SENT:
                place = st.at[0 : total // (8 * CHIP)]
            else:
                place = kv.at[0 : total // (2 * HEAD)]
            remote(place, place, out_s.at[group], out_s.at[group], twin).wait_send()

    def arrived(dst, rsem):
        remote(dst, dst, rsem, rsem, twin).wait_recv()

    def same(a, b):
        return (a[0] - b[0]) % 4 == 0 and (a[1] - b[1]) % 4 == 0

    def hop_send(buf, group, rsem, flow, hop, step):
        for i, (source, part, way) in enumerate(FLOWS[flow][hop]):
            if same(step, source):
                place = buf.at[rows(source, part)]
                send(place, place, group, rsem.at[flow, FIRST[hop] + i], at(way))

    def relay(buf, group, rsem, flow, hop):
        for i, (source, part, way) in enumerate(FLOWS[flow][hop]):
            step = (source[0] - way[0], source[1] - way[1])
            arrived(buf.at[rows(step, part)], rsem.at[flow, FIRST[hop] + i])
            if hop < 3:
                hop_send(buf, group, rsem, flow, hop + 1, step)

    mine = pl.ds(pl.multiple_of(s * TOK, 32), TOK)
    half = pl.ds(pl.multiple_of(c * TOK, 32), TOK)
    other_half = pl.ds(pl.multiple_of(o * TOK, 32), TOK)
    local = []
    for h in range(2):
        local += [
            pltpu.make_async_copy(k_hbm.at[:, cols(h)], kvs.at[h, :, 0:HEAD], loc.at[3 * h]),
            pltpu.make_async_copy(v_hbm.at[:, cols(h)], kvs.at[h, :, HEAD : 2 * HEAD], loc.at[3 * h + 1]),
            pltpu.make_async_copy(q_hbm.at[:, cols(h)], qds.at[h, :, 0:HEAD], loc.at[3 * h + 2]),
        ]
    local += [
        pltpu.make_async_copy(w_hbm, wv, loc.at[6]),
        pltpu.make_async_copy(gy_hbm, gyc.at[half], loc.at[7]),
        pltpu.make_async_copy(w_hbm.at[:, cols(z, 512)], wc.at[z], loc.at[8]),
    ]
    for copy in local:
        copy.start()
    m[...] = jnp.full_like(m, NEG)
    for ref in (l, acc, dq, dk, dv):
        ref[...] = jnp.zeros_like(ref)

    barrier = pltpu.get_barrier_semaphore()
    peers = [twin, (twin[0], wrap(z + 1, N_Z)), (twin[0], wrap(z - 1, N_Z))]
    for way in (RIGHT, LEFT, DOWN, UP):
        peers.append((chip_at(way) * 2 + o, z))
    for d in (1, 2, 3):
        peers += [at((0, d)), at((d, 0))]
    for d in range(1, N_Z):
        peers.append((s, wrap(z + d, N_Z)))
    for peer in peers:
        pl.semaphore_signal(barrier, inc=1, device_id=peer, device_id_type=MESH)
    pl.semaphore_wait(barrier, len(peers))

    def first_send(buf, stage, group, rsem):
        for i, way in enumerate((RIGHT, LEFT, DOWN, UP)):
            for h in range(2):
                send(stage.at[h], buf.at[mine], group, rsem.at[c, i], (chip_at(way) * 2 + h, z))

    def own_send(buf, stage, group):
        send(stage.at[o], buf.at[mine], group, own_r.at[group], twin)
        own = pltpu.make_async_copy(stage.at[c], buf.at[mine], loc.at[9 + group])
        own.start()
        return own

    theirs = pl.ds(pl.multiple_of((s + 1 - 2 * c) * TOK, 32), TOK)
    for n in (0, 1, 3, 4):
        local[n].wait()
    first_send(kv, kvs, KV_SENT, kv_r)
    own_kv = own_send(kv, kvs, KV_SENT)
    for d in range(1, N_Z):
        far = wrap(z + d, N_Z)
        send(
            w_hbm.at[cols(c), cols(far, 512)], wc.at[z, cols(c)], W_SENT, wz_r.at[d - 1], (s, far)
        )
    send(gy_hbm, gyc.at[half], TWIN_SENT, sib_r.at[4], twin)

    local[6].wait()
    local[7].wait()
    d_own = dot_nt(gyc[half, :], wv[...]).astype(BF16)
    qds[0, :, HEAD : 2 * HEAD] = d_own[:, 0:HEAD]
    qds[1, :, HEAD : 2 * HEAD] = d_own[:, HEAD:]
    local[2].wait()
    local[5].wait()

    def block_pos(index):
        return order[index] * TOK

    def row_pos(chips):
        lane = lax.broadcasted_iota(jnp.int32, (1, CHIP), 1)
        parts = [
            jnp.where(lane < TOK, block_pos(2 * n), block_pos(2 * n + 1) - TOK) + lane for n in chips
        ]
        return jnp.concatenate(parts, axis=1)

    def col_pos(a):
        return lax.broadcasted_iota(jnp.int32, (TOK, 1), 0) + block_pos(2 * chip + a)

    def own_rows(a):
        return pl.ds(pl.multiple_of(chip * CHIP + a * TOK, 32), TOK)

    def chip_rows(n):
        return pl.ds(pl.multiple_of(n * CHIP, 128), CHIP)

    def forward(chips):
        keys = jnp.concatenate([kv[chip_rows(n), 0:HEAD] for n in chips], axis=0)
        values = jnp.concatenate([kv[chip_rows(n), HEAD : 2 * HEAD] for n in chips], axis=0)
        key_pos = row_pos(chips)
        for a in range(2):
            rs = slice(a * TOK, (a + 1) * TOK)
            scores = dot_nt(qd[own_rows(a), 0:HEAD], keys) * SCALE2
            scores = jnp.where(key_pos <= col_pos(a), scores, NEG)
            before = m[rs, 0:1]
            now = jnp.maximum(before, jnp.max(scores, axis=1, keepdims=True))
            factor = jnp.exp2(before - now)
            weights = jnp.exp2(scores - now)
            m[rs, :] = jnp.broadcast_to(now, (TOK, HEAD))
            total = weights[:, 0:HEAD]
            for t in range(1, weights.shape[1] // HEAD):
                total = total + weights[:, t * HEAD : (t + 1) * HEAD]
            l[rs, :] = l[rs, :] * factor + total
            acc[rs, :] = acc[rs, :] * factor + dot(weights.astype(BF16), values)

    def query_grad(chips):
        keys = jnp.concatenate([kv[chip_rows(n), 0:HEAD] for n in chips], axis=0)
        values = jnp.concatenate([kv[chip_rows(n), HEAD : 2 * HEAD] for n in chips], axis=0)
        key_pos = row_pos(chips)
        for a in range(2):
            rs = slice(a * TOK, (a + 1) * TOK)
            scores = dot_nt(qd[own_rows(a), 0:HEAD], keys) * SCALE2 - m[rs, 0:1]
            probs = jnp.exp2(jnp.where(key_pos <= col_pos(a), scores, NEG))
            slopes = dot_nt(qd[own_rows(a), HEAD : 2 * HEAD], values)
            dscore = (probs * (slopes - l[rs, 0:1])).astype(BF16)
            dq[rs, :] += dot(dscore, keys)

    def key_grad(chips, halves=(0, 1)):
        queries = jnp.concatenate([qd[chip_rows(n), 0:HEAD] for n in chips], axis=0)
        douts = jnp.concatenate([qd[chip_rows(n), HEAD : 2 * HEAD] for n in chips], axis=0)
        query_pos = row_pos(chips)
        norm = jnp.concatenate([st[n, 0:1, :] for n in chips], axis=1)
        delta = jnp.concatenate([st[n, 1:2, :] for n in chips], axis=1)
        for a in halves:
            rs = slice(a * TOK, (a + 1) * TOK) if isinstance(a, int) else pl.ds(pl.multiple_of(a * TOK, 32), TOK)
            scores = dot_nt(kv[own_rows(a), 0:HEAD], queries) * SCALE2 - norm
            probs = jnp.exp2(jnp.where(col_pos(a) <= query_pos, scores, NEG))
            dv[rs, :] += dot(probs.astype(BF16), douts)
            slopes = dot_nt(kv[own_rows(a), HEAD : 2 * HEAD], douts)
            dscore = (probs * (slopes - delta)).astype(BF16)
            dk[rs, :] += dot(dscore, queries)

    relay(kv, KV_SENT, kv_r, 0, 0)
    relay(kv, KV_SENT, kv_r, 1, 0)
    own_kv.wait()
    arrived(kv.at[theirs], own_r.at[0])
    own_qd = own_send(qd, qds, QD_SENT)
    own_qd.wait()
    arrived(qd.at[theirs], own_r.at[1])
    forward([chip_at(step) for step in GROUPS[0]])

    relay(kv, KV_SENT, kv_r, 0, 1)
    relay(kv, KV_SENT, kv_r, 1, 1)
    first_send(qd, qds, QD_SENT, qd_r)
    forward([chip_at(step) for step in GROUPS[1]])

    relay(kv, KV_SENT, kv_r, 0, 2)
    relay(kv, KV_SENT, kv_r, 1, 2)
    relay(qd, QD_SENT, qd_r, 0, 0)
    relay(qd, QD_SENT, qd_r, 1, 0)
    forward([chip_at(step) for step in GROUPS[2][:4]])
    relay(kv, KV_SENT, kv_r, 0, 3)
    relay(kv, KV_SENT, kv_r, 1, 3)
    forward([chip_at(step) for step in GROUPS[2][4:]])

    for a in range(2):
        rs = slice(a * TOK, (a + 1) * TOK)
        denominator = jnp.sum(l[rs, :], axis=1, keepdims=True)
        attention = (acc[rs, :] / denominator).astype(BF16)
        attb[rs, :] = attention
        grads = qd[own_rows(a), HEAD : 2 * HEAD].astype(F32)
        delta = jnp.sum(grads * attention.astype(F32), axis=1, keepdims=True)
        m[rs, :] = jnp.broadcast_to(m[rs, 0:1] + jnp.log2(denominator), (TOK, HEAD))
        l[rs, :] = jnp.broadcast_to(delta, (TOK, HEAD))
    lane = lax.broadcasted_iota(jnp.int32, (CHIP, HEAD), 1)
    st[chip] = jnp.transpose(jnp.where(lane == 0, m[...], l[...]))[0:8, :]

    for d in (1, 2, 3):
        send(st.at[chip], st.at[chip], ST_SENT, st_r.at[0, d - 1], at((0, d)))
    own_att = pltpu.make_async_copy(attb.at[half], ag.at[z, :, cols(c)], loc.at[11])
    own_att.start()
    for part in range(2):
        for n, step in enumerate((1, -1)):
            for h in range(2):
                send(
                    attb.at[h * TOK + part * HALF : h * TOK + (part + 1) * HALF],
                    ag.at[z, part * HALF : (part + 1) * HALF, cols(c)],
                    Z_SENT,
                    a0_r.at[2 * n + part, c],
                    (chip * 2 + h, wrap(z + step, N_Z)),
                )
    send(attb.at[other_half], ag.at[z, :, cols(c)], TWIN_SENT, sib_r.at[5], twin)

    arrived(gyc.at[other_half], sib_r.at[4])
    att_t = jnp.transpose(attb[...].astype(F32)).astype(BF16)

    @pl.loop(0, 4)
    def _(n):
        part = dot(att_t, gyc[:, pl.ds(pl.multiple_of(n * 1024, 1024), 1024)]).astype(BF16)
        for i in range(4):
            gb[n, i] = part[:, i * 256 : (i + 1) * 256]


    def z_at(step):
        return wrap(z + step, N_Z)

    def z_place(block, part):
        return ag.at[z_at(block), part * HALF : (part + 1) * HALF]

    def z_send(hop, way, part):
        place = z_place(-way * hop, part)
        n = way_index(way), 2 * hop + part
        send(place, place, Z_SENT, az_r.at[n], (s, z_at(way)))

    def way_index(way):
        return 0 if way > 0 else 1

    def z_relay(hop):
        for part in (0, 1):
            for way in (1, -1):
                if hop == 3 and part != way_index(way):
                    continue
                n = way_index(way), 2 * hop + part
                if hop == 0:
                    for h in range(2):
                        place = ag.at[z_at(-way), part * HALF : (part + 1) * HALF, cols(h)]
                        arrived(place, a0_r.at[2 * n[0] + part, h])
                else:
                    arrived(z_place(-way * (hop + 1), part), az_r.at[n])
                if hop < 2 or (hop == 2 and part == way_index(way)):
                    z_send(hop + 1, way, part)

    def axis_at(way, stage, d):
        return at((0, d)) if way == stage else at((d, 0))

    def slab(way, d, first, size):
        span = pl.ds(way * 64 + first, size)
        return gb.at[:, wrap(x + d, 4), span] if way == 0 else gb.at[wrap(y + d, 4), :, span]

    def second(way, d):
        return wrap((y if way == 0 else x) + d, 4)

    def added(first, *others):
        total = first.astype(F32)
        for other in others:
            total = total + other.astype(F32)
        return total

    def sum_far():
        for way in range(2):
            for n, d in enumerate((1, -1)):
                send(slab(way, 2, 32 * n, 32), ga.at[way, n], G_SENT, g_r.at[way, n], axis_at(way, 0, d))

    def sum_near():
        for way in range(2):
            for n, d in enumerate((1, -1)):
                arrived(ga.at[way, n], g_r.at[way, n])
                rest = slice(32 - 32 * n, 64 - 32 * n)
                gt[way, n, :, 32 * n : 32 * n + 32] = added(slab(way, d, 32 * n, 32)[...], ga[way, n]).astype(BF16)
                gt[way, n, :, rest] = slab(way, d, 32 - 32 * n, 32)[...]
                send(gt.at[way, n], gr.at[way, n], G_SENT, g_r.at[2 + way, n], axis_at(way, 0, d))

    def sum_far_again():
        for way in range(2):
            for n in range(2):
                arrived(gr.at[way, n], g_r.at[2 + way, n])
            h1[way] = added(slab(way, 0, 0, 64)[...], gr[way, 0], gr[way, 1]).astype(BF16)
            for n, d in enumerate((1, -1)):
                place = h1.at[way, second(way, 2), pl.ds(32 * n, 32)]
                send(place, ga2.at[way, n], G_SENT, g_r.at[4 + way, n], axis_at(way, 1, d))
            send(h1.at[way, second(way, 0), :, cols(o)], gswap.at[way], G_SENT, sib_r.at[way], twin)

    def sum_near_again():
        for way in range(2):
            for n, d in enumerate((1, -1)):
                arrived(ga2.at[way, n], g_r.at[4 + way, n])
                block = h1[way, second(way, d)]
                rest = slice(32 - 32 * n, 64 - 32 * n)
                gt2[way, n, 32 * n : 32 * n + 32] = added(block[32 * n : 32 * n + 32], ga2[way, n]).astype(BF16)
                gt2[way, n, rest] = block[rest]
                for h in range(2):
                    device = axis_at(way, 1, d)
                    device = (device[0] - c + h, z)
                    send(gt2.at[way, n, :, cols(h)], gr2.at[way, n, c], G_SENT, gw_r.at[2 * way + n, c], device)

    def sum_last():
        for way in range(2):
            arrived(gswap.at[way], sib_r.at[way])
            own = h1[way, second(way, 0)]
            own = jnp.where(c == 0, own[:, 0:HEAD], own[:, HEAD:])
            for h in range(2):
                for n in range(2):
                    arrived(gr2.at[way, n, h], gw_r.at[2 * way + n, h])
                total = added(jnp.where(c == h, own, gswap[way]), gr2[way, 0, h], gr2[way, 1, h])
                gw_ref[h * HEAD + way * 64 : h * HEAD + way * 64 + 64, :] = total.astype(BF16)

    sum_far()

    def st_row(step):
        return st.at[pl.ds(wrap(y + step, 4) * 4, 4)]

    def swap_send(n, ref, factor):
        swap[0, n] = (ref[other_half, :] * factor).astype(BF16)
        send(swap.at[0, n], swap.at[1, n], TWIN_SENT, sib_r.at[7 + n], twin)

    query_grad(list(range(0, 4)))
    relay(qd, QD_SENT, qd_r, 0, 1)
    relay(qd, QD_SENT, qd_r, 1, 1)
    z_relay(0)
    for d in (1, 2, 3):
        arrived(st.at[chip_at((0, -d))], st_r.at[0, d - 1])
    for d in (1, 2, 3):
        send(st_row(0), st_row(0), ST_SENT, st_r.at[1, d - 1], at((d, 0)))
    query_grad(list(range(4, 8)))
    sum_near()
    z_relay(1)
    for d in range(1, N_Z):
        place = wc.at[z_at(-d), cols(c)]
        arrived(place, wz_r.at[d - 1])
        send(place, place, W_SENT, ws_r.at[d - 1], twin)
    query_grad(list(range(8, 12)))
    relay(qd, QD_SENT, qd_r, 0, 2)
    relay(qd, QD_SENT, qd_r, 1, 2)
    z_relay(2)
    query_grad(list(range(12, 16)))
    sum_far_again()
    swap_send(0, dq, SCALE)
    for d in (1, 2, 3):
        arrived(st_row(-d), st_r.at[1, d - 1])
    key_grad([chip_at(step) for step in GROUPS[0]])
    sum_near_again()
    key_grad([chip_at(step) for step in GROUPS[1]])

    for d in range(1, N_Z):
        arrived(wc.at[z_at(-d), cols(o)], ws_r.at[d - 1])
    z_relay(3)
    local[8].wait()
    own_att.wait()
    arrived(ag.at[z, :, cols(o)], sib_r.at[5])
    total = dot(ag[0], wc[0])
    for n in range(1, N_Z):
        total = total + dot(ag[n], wc[n])
    out_ref[...] = total.astype(BF16)
    sum_last()

    key_grad([chip_at(step) for step in GROUPS[2][:4]])
    relay(qd, QD_SENT, qd_r, 0, 3)
    relay(qd, QD_SENT, qd_r, 1, 3)
    key_grad([chip_at(step) for step in GROUPS[2][4:]], (o,))
    swap_send(1, dk, SCALE)
    swap_send(2, dv, 1.0)
    key_grad([chip_at(step) for step in GROUPS[2][4:]], (c,))

    for n, (ref, total, factor) in enumerate(((dq_ref, dq, SCALE), (dk_ref, dk, SCALE), (dv_ref, dv, 1.0))):
        own = (total[half, :] * factor).astype(BF16)
        arrived(swap.at[1, n], sib_r.at[7 + n])
        other = swap[1, n]
        ref[:, 0:HEAD] = jnp.where(c == 0, own, other)
        ref[:, HEAD : 2 * HEAD] = jnp.where(c == 0, other, own)
    all_sent()


def copy_kernel(*refs):
    for n in range(5):
        refs[5 + n][...] = refs[n][...]


def shards(queries, key_states, value_states, w_out, grad_y, chain_order):
    anywhere = pl.BlockSpec(memory_space=pl.ANY)
    vmem = pl.BlockSpec(memory_space=pltpu.VMEM)
    dma = pltpu.SemaphoreType.DMA
    tokens = 32 * TOK
    tile = jax.ShapeDtypeStruct((TOK, 2 * HEAD), BF16)
    scratch = [
        pltpu.VMEM((tokens, 2 * HEAD), BF16),
        pltpu.VMEM((tokens, 2 * HEAD), BF16),
        pltpu.VMEM((2 * HEAD, 4096), BF16),
        pltpu.VMEM((CHIP, 4096), BF16),
        pltpu.VMEM((N_Z, 2 * HEAD, 512), BF16),
        pltpu.VMEM((N_Z, TOK, 2 * HEAD), BF16),
        pltpu.VMEM((4, 4, HEAD, 256), BF16),
        pltpu.VMEM((2, 2, 4, 32, 256), BF16),
        pltpu.VMEM((2, 2, 4, 64, 256), BF16),
        pltpu.VMEM((2, 2, 4, 64, 256), BF16),
        pltpu.VMEM((2, 4, 64, 256), BF16),
        pltpu.VMEM((2, 2, 32, 256), BF16),
        pltpu.VMEM((2, 2, 64, 256), BF16),
        pltpu.VMEM((2, 2, 2, 64, HEAD), BF16),
        pltpu.VMEM((16, 8, CHIP), F32),
        pltpu.VMEM((CHIP, HEAD), BF16),
        pltpu.VMEM((2, TOK, 2 * HEAD), BF16),
        pltpu.VMEM((2, TOK, 2 * HEAD), BF16),
        pltpu.VMEM((2, 3, TOK, HEAD), BF16),
        pltpu.VMEM((2, 64, HEAD), BF16),
    ]
    scratch += [pltpu.VMEM((CHIP, HEAD), F32)] * 6
    scratch += [dma((N_GROUPS,)), dma((2, N_COPIES)), dma((2, N_COPIES)), dma((2,)), dma((12,)), dma((10,))]
    scratch += [dma((7,)), dma((7,)), dma((2, 3)), dma((2, 8)), dma((4, 2)), dma((6, 2)), dma((4, 2))]
    results = pl.pallas_call(
        kernel,
        out_shape=(
            jax.ShapeDtypeStruct((TOK, 512), BF16),
            tile,
            tile,
            tile,
            jax.ShapeDtypeStruct((2 * HEAD, HEAD), BF16),
        ),
        in_specs=[anywhere] * 5 + [pl.BlockSpec(memory_space=pltpu.SMEM)],
        out_specs=(vmem,) * 5,
        scratch_shapes=scratch,
        compiler_params=pltpu.CompilerParams(
            collective_id=0, has_side_effects=True, vmem_limit_bytes=56 * 1024 * 1024
        ),
        name="attention_layer",
    )(queries, key_states, value_states, w_out, grad_y, chain_order)
    return pl.pallas_call(
        copy_kernel,
        out_shape=tuple(jax.ShapeDtypeStruct(r.shape, r.dtype) for r in results),
        in_specs=[vmem] * 5,
        out_specs=(vmem,) * 5,
        name="results",
    )(*results)


def solution(mesh):
    return jax.shard_map(
        shards,
        mesh=mesh,
        in_specs=(
            P("seq", "head"),
            P("seq", "head"),
            P("seq", "head"),
            P("head", None),
            P("seq", None),
            P(),
        ),
        out_specs=(
            P("seq", "head"),
            P("seq", "head"),
            P("seq", "head"),
            P("seq", "head"),
            P("head", "seq"),
        ),
        check_vma=False,
    )
```

```python
import math

import jax
import jax.numpy as jnp
from jax import lax
from jax.experimental import pallas as pl
from jax.experimental.pallas import tpu as pltpu
from jax.sharding import PartitionSpec as P

F32 = jnp.float32
BF16 = jnp.bfloat16
MESH = pl.DeviceIdType.MESH
HEAD = 128
TOK = 192
CHIP = 2 * TOK
HALF = TOK // 2
N_Z = 8
SCALE = 1.0 / math.sqrt(HEAD)
SCALE2 = SCALE * math.log2(math.e)
NEG = -1e30

RIGHT, LEFT, DOWN, UP = (0, 1), (0, -1), (1, 0), (-1, 0)
EVEN, ODD = (0, TOK), (TOK, TOK)
EVEN_TOP, EVEN_LOW = (0, HALF), (HALF, HALF)
ODD_TOP, ODD_LOW = (TOK, HALF), (TOK + HALF, HALF)
WHOLE = (0, CHIP)

FLOWS = [
    [
        [((0, 0), EVEN, d) for d in (RIGHT, LEFT, DOWN, UP)],
        [
            ((0, -1), EVEN, DOWN),
            ((0, -1), EVEN, UP),
            ((0, -1), EVEN, RIGHT),
            ((0, 1), EVEN, DOWN),
            ((0, 1), EVEN, UP),
            ((-1, 0), EVEN, DOWN),
        ],
        [
            ((0, 2), EVEN, DOWN),
            ((0, 2), EVEN, UP),
            ((-1, -1), EVEN_TOP, DOWN),
            ((-1, 1), EVEN_TOP, DOWN),
            ((1, -1), EVEN_LOW, UP),
            ((1, 1), EVEN_LOW, UP),
        ],
        [((-1, 2), EVEN_TOP, DOWN), ((1, 2), EVEN_LOW, UP)],
    ],
    [
        [((0, 0), ODD, d) for d in (RIGHT, LEFT, DOWN, UP)],
        [
            ((1, 0), ODD, RIGHT),
            ((1, 0), ODD, LEFT),
            ((1, 0), ODD, UP),
            ((-1, 0), ODD, RIGHT),
            ((-1, 0), ODD, LEFT),
            ((0, 1), ODD, LEFT),
        ],
        [
            ((2, 0), ODD, RIGHT),
            ((2, 0), ODD, LEFT),
            ((-1, -1), ODD_TOP, RIGHT),
            ((1, -1), ODD_TOP, RIGHT),
            ((-1, 1), ODD_LOW, LEFT),
            ((1, 1), ODD_LOW, LEFT),
        ],
        [((2, -1), ODD_TOP, RIGHT), ((2, 1), ODD_LOW, LEFT)],
    ],
]
FIRST = [0, 4, 10, 16]
N_COPIES = 18
KV_SENT, QD_SENT, W_SENT, Z_SENT, TWIN_SENT, G_SENT, ST_SENT = range(7)
N_GROUPS = 7
GROUPS = [
    [(0, 0), (0, -1), (0, 1), (-1, 0), (1, 0)],
    [(0, 2), (2, 0), (-1, -1), (-1, 1), (1, -1), (1, 1)],
    [(-1, 2), (1, 2), (2, -1), (2, 1), (2, 2)],
]


def dot(a, b):
    return jnp.dot(a, b, preferred_element_type=F32)


def dot_nt(a, b):
    return lax.dot_general(a, b, (((1,), (1,)), ((), ())), preferred_element_type=F32)


def wrap(value, size):
    return lax.rem(value + 2 * size, size)


def kernel(
    q_hbm, k_hbm, v_hbm, w_hbm, gy_hbm, order,
    out_ref, dq_ref, dk_ref, dv_ref, gw_ref,
    kv, qd, wv, gyc, wc, ag, gb, ga, gt, gr, h1, ga2, gt2, gr2, st, attb, kvs, qds, swap, gswap,
    m, l, ds, dl, dq, dk, dv, acc,
    out_s, kv_r, qd_r, own_r, loc, sib_r, wz_r, ws_r, st_r, az_r, a0_r, g_r, gw_r,
):
    s = lax.axis_index("seq")
    z = lax.axis_index("head")
    y = s // 8
    x = lax.rem(s // 2, 4)
    c = lax.rem(s, 2)
    chip = y * 4 + x
    twin = (s + 1 - 2 * c, z)
    o = 1 - c

    def at(step):
        return ((wrap(y + step[0], 4) * 4 + wrap(x + step[1], 4)) * 2 + c, z)

    def chip_at(step):
        return wrap(y + step[0], 4) * 4 + wrap(x + step[1], 4)

    def rows(step, part=WHOLE):
        return pl.ds(pl.multiple_of(chip_at(step) * CHIP + part[0], 32), part[1])

    def cols(index, size=HEAD):
        return pl.ds(pl.multiple_of(index * size, size), size)

    def remote(src, dst, send, recv, device):
        return pltpu.make_async_remote_copy(
            src_ref=src, dst_ref=dst, send_sem=send, recv_sem=recv, device_id=device, device_id_type=MESH
        )

    totals = [0] * N_GROUPS

    def send(src, dst, group, rsem, device):
        remote(src, dst, out_s.at[group], rsem, device).start()
        totals[group] += math.prod(src.shape)

    def all_sent():
        for group, total in enumerate(totals):
            if group == ST_SENT:
                place = st.at[0 : total // (8 * CHIP)]
            else:
                place = kv.at[0 : total // (2 * HEAD)]
            remote(place, place, out_s.at[group], out_s.at[group], twin).wait_send()

    def arrived(dst, rsem):
        remote(dst, dst, rsem, rsem, twin).wait_recv()

    def same(a, b):
        return (a[0] - b[0]) % 4 == 0 and (a[1] - b[1]) % 4 == 0

    def hop_send(buf, group, rsem, flow, hop, step):
        for i, (source, part, way) in enumerate(FLOWS[flow][hop]):
            if same(step, source):
                place = buf.at[rows(source, part)]
                send(place, place, group, rsem.at[flow, FIRST[hop] + i], at(way))

    def relay(buf, group, rsem, flow, hop):
        for i, (source, part, way) in enumerate(FLOWS[flow][hop]):
            step = (source[0] - way[0], source[1] - way[1])
            arrived(buf.at[rows(step, part)], rsem.at[flow, FIRST[hop] + i])
            if hop < 3:
                hop_send(buf, group, rsem, flow, hop + 1, step)

    mine = pl.ds(pl.multiple_of(s * TOK, 32), TOK)
    half = pl.ds(pl.multiple_of(c * TOK, 32), TOK)
    other_half = pl.ds(pl.multiple_of(o * TOK, 32), TOK)
    local = []
    for h in range(2):
        local += [
            pltpu.make_async_copy(k_hbm.at[:, cols(h)], kvs.at[h, :, 0:HEAD], loc.at[3 * h]),
            pltpu.make_async_copy(v_hbm.at[:, cols(h)], kvs.at[h, :, HEAD : 2 * HEAD], loc.at[3 * h + 1]),
            pltpu.make_async_copy(q_hbm.at[:, cols(h)], qds.at[h, :, 0:HEAD], loc.at[3 * h + 2]),
        ]
    local += [
        pltpu.make_async_copy(w_hbm, wv, loc.at[6]),
        pltpu.make_async_copy(gy_hbm, gyc.at[half], loc.at[7]),
        pltpu.make_async_copy(w_hbm.at[:, cols(z, 512)], wc.at[z], loc.at[8]),
    ]
    for copy in local:
        copy.start()
    m[...] = jnp.full_like(m, NEG)
    for ref in (l, ds, dl, dq, dk, dv, acc):
        ref[...] = jnp.zeros_like(ref)

    barrier = pltpu.get_barrier_semaphore()
    peers = [twin, (twin[0], wrap(z + 1, N_Z)), (twin[0], wrap(z - 1, N_Z))]
    for way in (RIGHT, LEFT, DOWN, UP):
        peers.append((chip_at(way) * 2 + o, z))
    for d in (1, 2, 3):
        peers += [at((0, d)), at((d, 0))]
    for d in range(1, N_Z):
        peers.append((s, wrap(z + d, N_Z)))
    for peer in peers:
        pl.semaphore_signal(barrier, inc=1, device_id=peer, device_id_type=MESH)
    pl.semaphore_wait(barrier, len(peers))

    def first_send(buf, stage, group, rsem):
        for i, way in enumerate((RIGHT, LEFT, DOWN, UP)):
            for h in range(2):
                send(stage.at[h], buf.at[mine], group, rsem.at[c, i], (chip_at(way) * 2 + h, z))

    def own_send(buf, stage, group):
        send(stage.at[o], buf.at[mine], group, own_r.at[group], twin)
        own = pltpu.make_async_copy(stage.at[c], buf.at[mine], loc.at[9 + group])
        own.start()
        return own

    theirs = pl.ds(pl.multiple_of((s + 1 - 2 * c) * TOK, 32), TOK)
    for n in (0, 1, 3, 4):
        local[n].wait()
    first_send(kv, kvs, KV_SENT, kv_r)
    own_kv = own_send(kv, kvs, KV_SENT)
    for d in range(1, N_Z):
        far = wrap(z + d, N_Z)
        send(
            w_hbm.at[cols(c), cols(far, 512)], wc.at[z, cols(c)], W_SENT, wz_r.at[d - 1], (s, far)
        )
    send(gy_hbm, gyc.at[half], TWIN_SENT, sib_r.at[4], twin)

    local[6].wait()
    local[7].wait()
    d_own = dot_nt(gyc[half, :], wv[...]).astype(BF16)
    qds[0, :, HEAD : 2 * HEAD] = d_own[:, 0:HEAD]
    qds[1, :, HEAD : 2 * HEAD] = d_own[:, HEAD:]
    local[2].wait()
    local[5].wait()

    def block_pos(index):
        return order[index] * TOK

    def row_pos(chips):
        lane = lax.broadcasted_iota(jnp.int32, (1, CHIP), 1)
        parts = [
            jnp.where(lane < TOK, block_pos(2 * n), block_pos(2 * n + 1) - TOK) + lane for n in chips
        ]
        return jnp.concatenate(parts, axis=1)

    def col_pos(a):
        return lax.broadcasted_iota(jnp.int32, (TOK, 1), 0) + block_pos(2 * chip + a)

    def own_rows(a):
        return pl.ds(pl.multiple_of(chip * CHIP + a * TOK, 32), TOK)

    def chip_rows(n):
        return pl.ds(pl.multiple_of(n * CHIP, 128), CHIP)

    def lanes(wide):
        total = wide[:, 0:HEAD]
        for t in range(1, wide.shape[1] // HEAD):
            total = total + wide[:, t * HEAD : (t + 1) * HEAD]
        return total

    def forward(chips):
        blocks = jnp.concatenate([kv[chip_rows(n), :] for n in chips], axis=0)
        keys, values = blocks[:, 0:HEAD], blocks[:, HEAD:]
        key_pos = row_pos(chips)
        for a in range(2):
            rs = slice(a * TOK, (a + 1) * TOK)
            scores = dot_nt(qd[own_rows(a), 0:HEAD], keys) * SCALE2
            scores = jnp.where(key_pos <= col_pos(a), scores, NEG)
            before = m[rs, 0:1]
            now = jnp.maximum(before, jnp.max(scores, axis=1, keepdims=True))
            factor = jnp.exp2(before - now)
            weights = jnp.exp2(scores - now)
            m[rs, :] = jnp.broadcast_to(now, (TOK, HEAD))
            slopes = dot_nt(qd[own_rows(a), HEAD : 2 * HEAD], values)
            norms = l[rs, :] * factor + lanes(weights)
            deltas = ds[rs, :] * factor + lanes(weights * slopes)
            l[rs, :] = norms
            ds[rs, :] = deltas
            delta = jnp.sum(deltas, axis=1, keepdims=True) / jnp.sum(norms, axis=1, keepdims=True)
            moved = delta - dl[rs, 0:1]
            dl[rs, :] = jnp.broadcast_to(delta, (TOK, HEAD))
            old = acc[rs, :] * factor
            dscore = (weights * (slopes - delta)).astype(BF16)
            dq[rs, :] = dq[rs, :] * factor - moved * old[:, 0:HEAD] + dot(dscore, keys)
            acc[rs, :] = old + dot(weights.astype(BF16), blocks)

    def key_grad(chips, halves=(0, 1)):
        queries = jnp.concatenate([qd[chip_rows(n), 0:HEAD] for n in chips], axis=0)
        douts = jnp.concatenate([qd[chip_rows(n), HEAD : 2 * HEAD] for n in chips], axis=0)
        query_pos = row_pos(chips)
        norm = jnp.concatenate([st[n, 0:1, :] for n in chips], axis=1)
        delta = jnp.concatenate([st[n, 1:2, :] for n in chips], axis=1)
        for a in halves:
            rs = slice(a * TOK, (a + 1) * TOK) if isinstance(a, int) else pl.ds(pl.multiple_of(a * TOK, 32), TOK)
            scores = dot_nt(kv[own_rows(a), 0:HEAD], queries) * SCALE2 - norm
            probs = jnp.exp2(jnp.where(col_pos(a) <= query_pos, scores, NEG))
            dv[rs, :] += dot(probs.astype(BF16), douts)
            slopes = dot_nt(kv[own_rows(a), HEAD : 2 * HEAD], douts)
            dscore = (probs * (slopes - delta)).astype(BF16)
            dk[rs, :] += dot(dscore, queries)

    relay(kv, KV_SENT, kv_r, 0, 0)
    relay(kv, KV_SENT, kv_r, 1, 0)
    own_kv.wait()
    arrived(kv.at[theirs], own_r.at[0])
    own_qd = own_send(qd, qds, QD_SENT)
    own_qd.wait()
    arrived(qd.at[theirs], own_r.at[1])
    forward([chip_at(step) for step in GROUPS[0]])

    relay(kv, KV_SENT, kv_r, 0, 1)
    relay(kv, KV_SENT, kv_r, 1, 1)
    first_send(qd, qds, QD_SENT, qd_r)
    forward([chip_at(step) for step in GROUPS[1]])

    relay(kv, KV_SENT, kv_r, 0, 2)
    relay(kv, KV_SENT, kv_r, 1, 2)
    relay(qd, QD_SENT, qd_r, 0, 0)
    relay(qd, QD_SENT, qd_r, 1, 0)
    forward([chip_at(step) for step in GROUPS[2][:4]])
    relay(kv, KV_SENT, kv_r, 0, 3)
    relay(kv, KV_SENT, kv_r, 1, 3)
    forward([chip_at(step) for step in GROUPS[2][4:]])

    for a in range(2):
        rs = slice(a * TOK, (a + 1) * TOK)
        denominator = jnp.sum(l[rs, :], axis=1, keepdims=True)
        attention = (acc[rs, HEAD:] / denominator).astype(BF16)
        attb[rs, :] = attention
        grads = qd[own_rows(a), HEAD : 2 * HEAD].astype(F32)
        delta = jnp.sum(grads * attention.astype(F32), axis=1, keepdims=True)
        dq[rs, :] = (dq[rs, :] - (delta - dl[rs, 0:1]) * acc[rs, 0:HEAD]) / denominator
        m[rs, :] = jnp.broadcast_to(m[rs, 0:1] + jnp.log2(denominator), (TOK, HEAD))
        l[rs, :] = jnp.broadcast_to(delta, (TOK, HEAD))
    lane = lax.broadcasted_iota(jnp.int32, (CHIP, HEAD), 1)
    st[chip] = jnp.transpose(jnp.where(lane == 0, m[...], l[...]))[0:8, :]

    for d in (1, 2, 3):
        send(st.at[chip], st.at[chip], ST_SENT, st_r.at[0, d - 1], at((0, d)))
    own_att = pltpu.make_async_copy(attb.at[half], ag.at[z, :, cols(c)], loc.at[11])
    own_att.start()
    for part in range(2):
        for n, step in enumerate((1, -1)):
            for h in range(2):
                send(
                    attb.at[h * TOK + part * HALF : h * TOK + (part + 1) * HALF],
                    ag.at[z, part * HALF : (part + 1) * HALF, cols(c)],
                    Z_SENT,
                    a0_r.at[2 * n + part, c],
                    (chip * 2 + h, wrap(z + step, N_Z)),
                )
    send(attb.at[other_half], ag.at[z, :, cols(c)], TWIN_SENT, sib_r.at[5], twin)

    arrived(gyc.at[other_half], sib_r.at[4])
    att_t = jnp.transpose(attb[...].astype(F32)).astype(BF16)

    @pl.loop(0, 4)
    def _(n):
        part = dot(att_t, gyc[:, pl.ds(pl.multiple_of(n * 1024, 1024), 1024)]).astype(BF16)
        for i in range(4):
            gb[n, i] = part[:, i * 256 : (i + 1) * 256]


    def z_at(step):
        return wrap(z + step, N_Z)

    def z_place(block, part):
        return ag.at[z_at(block), part * HALF : (part + 1) * HALF]

    def z_send(hop, way, part):
        place = z_place(-way * hop, part)
        n = way_index(way), 2 * hop + part
        send(place, place, Z_SENT, az_r.at[n], (s, z_at(way)))

    def way_index(way):
        return 0 if way > 0 else 1

    def z_relay(hop):
        for part in (0, 1):
            for way in (1, -1):
                if hop == 3 and part != way_index(way):
                    continue
                n = way_index(way), 2 * hop + part
                if hop == 0:
                    for h in range(2):
                        place = ag.at[z_at(-way), part * HALF : (part + 1) * HALF, cols(h)]
                        arrived(place, a0_r.at[2 * n[0] + part, h])
                else:
                    arrived(z_place(-way * (hop + 1), part), az_r.at[n])
                if hop < 2 or (hop == 2 and part == way_index(way)):
                    z_send(hop + 1, way, part)

    def axis_at(way, stage, d):
        return at((0, d)) if way == stage else at((d, 0))

    def slab(way, d, first, size):
        span = pl.ds(way * 64 + first, size)
        return gb.at[:, wrap(x + d, 4), span] if way == 0 else gb.at[wrap(y + d, 4), :, span]

    def second(way, d):
        return wrap((y if way == 0 else x) + d, 4)

    def added(first, *others):
        total = first.astype(F32)
        for other in others:
            total = total + other.astype(F32)
        return total

    def sum_far():
        for way in range(2):
            for n, d in enumerate((1, -1)):
                send(slab(way, 2, 32 * n, 32), ga.at[way, n], G_SENT, g_r.at[way, n], axis_at(way, 0, d))

    def sum_near():
        for way in range(2):
            for n, d in enumerate((1, -1)):
                arrived(ga.at[way, n], g_r.at[way, n])
                rest = slice(32 - 32 * n, 64 - 32 * n)
                gt[way, n, :, 32 * n : 32 * n + 32] = added(slab(way, d, 32 * n, 32)[...], ga[way, n]).astype(BF16)
                gt[way, n, :, rest] = slab(way, d, 32 - 32 * n, 32)[...]
                send(gt.at[way, n], gr.at[way, n], G_SENT, g_r.at[2 + way, n], axis_at(way, 0, d))

    def sum_far_again():
        for way in range(2):
            for n in range(2):
                arrived(gr.at[way, n], g_r.at[2 + way, n])
            h1[way] = added(slab(way, 0, 0, 64)[...], gr[way, 0], gr[way, 1]).astype(BF16)
            for n, d in enumerate((1, -1)):
                place = h1.at[way, second(way, 2), pl.ds(32 * n, 32)]
                send(place, ga2.at[way, n], G_SENT, g_r.at[4 + way, n], axis_at(way, 1, d))
            send(h1.at[way, second(way, 0), :, cols(o)], gswap.at[way], G_SENT, sib_r.at[way], twin)

    def sum_near_again():
        for way in range(2):
            for n, d in enumerate((1, -1)):
                arrived(ga2.at[way, n], g_r.at[4 + way, n])
                block = h1[way, second(way, d)]
                rest = slice(32 - 32 * n, 64 - 32 * n)
                gt2[way, n, 32 * n : 32 * n + 32] = added(block[32 * n : 32 * n + 32], ga2[way, n]).astype(BF16)
                gt2[way, n, rest] = block[rest]
                for h in range(2):
                    device = axis_at(way, 1, d)
                    device = (device[0] - c + h, z)
                    send(gt2.at[way, n, :, cols(h)], gr2.at[way, n, c], G_SENT, gw_r.at[2 * way + n, c], device)

    def sum_last():
        for way in range(2):
            arrived(gswap.at[way], sib_r.at[way])
            own = h1[way, second(way, 0)]
            own = jnp.where(c == 0, own[:, 0:HEAD], own[:, HEAD:])
            for h in range(2):
                for n in range(2):
                    arrived(gr2.at[way, n, h], gw_r.at[2 * way + n, h])
                total = added(jnp.where(c == h, own, gswap[way]), gr2[way, 0, h], gr2[way, 1, h])
                gw_ref[h * HEAD + way * 64 : h * HEAD + way * 64 + 64, :] = total.astype(BF16)

    sum_far()

    def st_row(step):
        return st.at[pl.ds(wrap(y + step, 4) * 4, 4)]

    def swap_send(n, ref, factor):
        swap[0, n] = (ref[other_half, :] * factor).astype(BF16)
        send(swap.at[0, n], swap.at[1, n], TWIN_SENT, sib_r.at[7 + n], twin)

    swap_send(0, dq, SCALE)
    relay(qd, QD_SENT, qd_r, 0, 1)
    relay(qd, QD_SENT, qd_r, 1, 1)
    for d in (1, 2, 3):
        arrived(st.at[chip_at((0, -d))], st_r.at[0, d - 1])
    for d in (1, 2, 3):
        send(st_row(0), st_row(0), ST_SENT, st_r.at[1, d - 1], at((d, 0)))
    z_relay(0)
    sum_near()
    for d in range(1, N_Z):
        place = wc.at[z_at(-d), cols(c)]
        arrived(place, wz_r.at[d - 1])
        send(place, place, W_SENT, ws_r.at[d - 1], twin)
    for d in (1, 2, 3):
        arrived(st_row(-d), st_r.at[1, d - 1])
    key_grad([chip_at(step) for step in GROUPS[0]])
    z_relay(1)
    relay(qd, QD_SENT, qd_r, 0, 2)
    relay(qd, QD_SENT, qd_r, 1, 2)
    sum_far_again()
    key_grad([chip_at(step) for step in GROUPS[1]])
    z_relay(2)
    sum_near_again()
    key_grad([chip_at(step) for step in GROUPS[2][:4]])

    relay(qd, QD_SENT, qd_r, 0, 3)
    relay(qd, QD_SENT, qd_r, 1, 3)
    key_grad([chip_at(step) for step in GROUPS[2][4:]], (o,))
    swap_send(1, dk, SCALE)
    swap_send(2, dv, 1.0)
    key_grad([chip_at(step) for step in GROUPS[2][4:]], (c,))

    for d in range(1, N_Z):
        arrived(wc.at[z_at(-d), cols(o)], ws_r.at[d - 1])
    z_relay(3)
    local[8].wait()
    own_att.wait()
    arrived(ag.at[z, :, cols(o)], sib_r.at[5])
    total = dot(ag[0], wc[0])
    for n in range(1, N_Z):
        total = total + dot(ag[n], wc[n])
    out_ref[...] = total.astype(BF16)
    sum_last()

    for n, (ref, total, factor) in enumerate(((dq_ref, dq, SCALE), (dk_ref, dk, SCALE), (dv_ref, dv, 1.0))):
        own = (total[half, :] * factor).astype(BF16)
        arrived(swap.at[1, n], sib_r.at[7 + n])
        other = swap[1, n]
        ref[:, 0:HEAD] = jnp.where(c == 0, own, other)
        ref[:, HEAD : 2 * HEAD] = jnp.where(c == 0, other, own)
    all_sent()


def copy_kernel(*refs):
    for n in range(5):
        refs[5 + n][...] = refs[n][...]


def shards(queries, key_states, value_states, w_out, grad_y, chain_order):
    anywhere = pl.BlockSpec(memory_space=pl.ANY)
    vmem = pl.BlockSpec(memory_space=pltpu.VMEM)
    dma = pltpu.SemaphoreType.DMA
    tokens = 32 * TOK
    tile = jax.ShapeDtypeStruct((TOK, 2 * HEAD), BF16)
    scratch = [
        pltpu.VMEM((tokens, 2 * HEAD), BF16),
        pltpu.VMEM((tokens, 2 * HEAD), BF16),
        pltpu.VMEM((2 * HEAD, 4096), BF16),
        pltpu.VMEM((CHIP, 4096), BF16),
        pltpu.VMEM((N_Z, 2 * HEAD, 512), BF16),
        pltpu.VMEM((N_Z, TOK, 2 * HEAD), BF16),
        pltpu.VMEM((4, 4, HEAD, 256), BF16),
        pltpu.VMEM((2, 2, 4, 32, 256), BF16),
        pltpu.VMEM((2, 2, 4, 64, 256), BF16),
        pltpu.VMEM((2, 2, 4, 64, 256), BF16),
        pltpu.VMEM((2, 4, 64, 256), BF16),
        pltpu.VMEM((2, 2, 32, 256), BF16),
        pltpu.VMEM((2, 2, 64, 256), BF16),
        pltpu.VMEM((2, 2, 2, 64, HEAD), BF16),
        pltpu.VMEM((16, 8, CHIP), F32),
        pltpu.VMEM((CHIP, HEAD), BF16),
        pltpu.VMEM((2, TOK, 2 * HEAD), BF16),
        pltpu.VMEM((2, TOK, 2 * HEAD), BF16),
        pltpu.VMEM((2, 3, TOK, HEAD), BF16),
        pltpu.VMEM((2, 64, HEAD), BF16),
    ]
    scratch += [pltpu.VMEM((CHIP, HEAD), F32)] * 7
    scratch += [pltpu.VMEM((CHIP, 2 * HEAD), F32)]
    scratch += [dma((N_GROUPS,)), dma((2, N_COPIES)), dma((2, N_COPIES)), dma((2,)), dma((12,)), dma((10,))]
    scratch += [dma((7,)), dma((7,)), dma((2, 3)), dma((2, 8)), dma((4, 2)), dma((6, 2)), dma((4, 2))]
    results = pl.pallas_call(
        kernel,
        out_shape=(
            jax.ShapeDtypeStruct((TOK, 512), BF16),
            tile,
            tile,
            tile,
            jax.ShapeDtypeStruct((2 * HEAD, HEAD), BF16),
        ),
        in_specs=[anywhere] * 5 + [pl.BlockSpec(memory_space=pltpu.SMEM)],
        out_specs=(vmem,) * 5,
        scratch_shapes=scratch,
        compiler_params=pltpu.CompilerParams(
            collective_id=0, has_side_effects=True, vmem_limit_bytes=56 * 1024 * 1024
        ),
        name="attention_layer",
    )(queries, key_states, value_states, w_out, grad_y, chain_order)
    return pl.pallas_call(
        copy_kernel,
        out_shape=tuple(jax.ShapeDtypeStruct(r.shape, r.dtype) for r in results),
        in_specs=[vmem] * 5,
        out_specs=(vmem,) * 5,
        name="results",
    )(*results)


def solution(mesh):
    return jax.shard_map(
        shards,
        mesh=mesh,
        in_specs=(
            P("seq", "head"),
            P("seq", "head"),
            P("seq", "head"),
            P("head", None),
            P("seq", None),
            P(),
        ),
        out_specs=(
            P("seq", "head"),
            P("seq", "head"),
            P("seq", "head"),
            P("seq", "head"),
            P("head", "seq"),
        ),
        check_vma=False,
    )
```
